256 devices in a mesh: cols: 32 (over y, x, core), rows: 8 (over z).
Axes of the slice: x: 4, y: 4, z: 8, core: 2. Of those that a mesh axis runs over, the one named last changes fastest.
Arguments:
- panel: bfloat16 [16, 96, 1024, 128], P('rows', 'cols'), may hold values from -0.1875 to 0.1875
- row_k: bfloat16 [96, 1024, 128], P('cols', 'rows'), as said below
- mask: int32 [16, 96], P('rows', 'cols'), may hold values 0 or 1
- a_low: bfloat16 [16, 1024, 128], P('rows'), may hold values from -0.375 to 0.375
- a_diag: float32 [1024, 1024], P('rows'), as said below
- sketch: bfloat16 [1024, 64], replicated, may hold values from -6 to 6
Outputs:
- panel_out: float32 [16, 1024, 128], P('rows')
- diag_factor: float32 [1024, 1024], P('rows')
The draws below stay inside these ranges and needn't reach their ends.
Inputs may be any that keep to these rules, and one draw needn't show every extreme that they name: row_k entries are normal with deviation 1024 ** -0.5, cut at six deviations. a_diag - update is symmetric, with every eigenvalue 2 or more.
All inputs are finite; a program needn't handle non-finite values. No bound on the sum of `mask` on one device may be relied on, other than what follows from the above.
Results may differ from the reference program's by a relative error of at most 0.02.
Values may be sent and summed in bfloat16 or wider, within the bound.
A program may use at most 128 MiB of HBM per device.

```python
import jax
import jax.numpy as jnp
from jax import lax

B = 1024
R = 64
P_SIZE = 64
TR_TOT = 16
JTOT = 96


def row_values(key):
    base = jax.random.fold_in(key, 101)
    values = jax.random.normal(base, (JTOT, B, 2 * R), jnp.float32)
    values = jnp.clip(values, -6.0, 6.0) * jnp.float32(B) ** (-0.5)
    return values.astype(jnp.bfloat16)


def draw_row_k(key, part):
    return row_values(key)


def draw_a_diag(key, part):
    factors = row_values(key).astype(jnp.float32)
    k_left = factors[..., :R]
    k_right = factors[..., R:]
    high = lax.Precision.HIGHEST
    diag_core = jnp.einsum('jbr,jbs->jrs', k_right, k_right, precision=high).astype(jnp.bfloat16).astype(jnp.float32)
    k_mixed = jnp.einsum('jbr,jrs->jbs', k_left, diag_core, precision=high).astype(jnp.bfloat16).astype(jnp.float32)
    update = jnp.einsum('jbs,jcs->bc', k_mixed, k_left, precision=high)
    mixing = jnp.clip(jax.random.normal(jax.random.fold_in(key, 202), (B, B), jnp.float32), -6.0, 6.0)
    covar = jnp.einsum('bk,ck->bc', mixing, mixing, precision=high) / jnp.float32(B)
    covar = 0.5 * (covar + covar.T)
    return 2.0 * jnp.eye(B, dtype=jnp.float32) + covar + update


def touch_ends(drawn, key, least, high):
    index_at = [jax.random.randint(jax.random.fold_in(key, axis), (), 0, length) for axis, length in enumerate(drawn.shape)]
    longest = drawn.shape.index(max(drawn.shape))
    beside = index_at[:longest] + [(index_at[longest] + 1) % drawn.shape[longest]] + index_at[longest + 1:]
    return drawn.at[tuple(index_at)].set(least).at[tuple(beside)].set(high)


def shard_levels(stream_key, dims, cuts, least, high):
    loudness = 1.0
    for dim, shards_of in cuts:
        draws = jax.random.uniform(jax.random.fold_in(jax.random.fold_in(stream_key, 6), dim), (shards_of,), jnp.float32, least / len(cuts), high / len(cuts))
        loudness = loudness * jnp.repeat(jnp.exp(draws), dims[dim] // shards_of).reshape((-1,) + (1,) * (len(dims) - 1 - dim))
    return loudness


def noise(own_key, shape, scale, reach, cuts=(), kind=jnp.bfloat16):
    entries = jax.random.normal(own_key, shape, jnp.float32) * scale
    if len(cuts) > 0:
        entries = shard_levels(own_key, shape, cuts, -0.22, 0.18) * entries
    return jnp.clip(entries, min=-reach, max=reach).astype(kind)


def setup_inputs(seed: int = 0) -> dict:
    seeds = jax.random.split(jax.random.key(seed), 7)
    return {
        "panel": noise(seeds[0], (TR_TOT, JTOT, B, 2 * R), B ** -0.5, 0.1875, ((0, 8), (1, 32))),
        "row_k": draw_row_k(jax.random.fold_in(seeds[6], 71), 0),
        "mask": touch_ends((jax.random.randint(seeds[2], (TR_TOT, JTOT), 0, 4) < 3).astype(jnp.int32), jax.random.fold_in(seeds[2], 1), 0, 1),
        "a_low": noise(seeds[3], (TR_TOT, B, 2 * R), (4 * R) ** -0.5, 0.375, ((0, 8),)),
        "a_diag": draw_a_diag(jax.random.fold_in(seeds[6], 71), 0),
        "sketch": noise(seeds[5], (B, P_SIZE), 1.0, 6.0),
    }


def mult(form, first, second):
    return jnp.einsum(form, first.astype(jnp.float32), second.astype(jnp.float32), precision=lax.Precision.HIGHEST)

def round_half(values):
    return lax.optimization_barrier(values.astype(jnp.bfloat16)).astype(jnp.float32)

def orthonormal(field):
    gram_matrix = mult('bp,bq->pq', field, field)
    lower_factor = jnp.linalg.cholesky(gram_matrix)
    return lax.linalg.triangular_solve(lower_factor, field.T, left_side=True, lower=True).T

def reference(panel, row_k, mask, a_low, a_diag, sketch):
    k_left = row_k[..., :R].astype(jnp.float32)
    k_right = row_k[..., R:].astype(jnp.float32)
    diag_core = round_half(mult('jbr,jbs->jrs', k_right, k_right))
    k_mixed = round_half(mult('jbr,jrs->jbs', k_left, diag_core))
    update = mult('jbs,jcs->bc', k_mixed, k_left)
    factor = jnp.linalg.cholesky(a_diag - update)
    omega = sketch.astype(jnp.float32)
    probe = round_half(mult('jbr,bp->jrp', k_left, omega))

    def one_row(items):
        tiles, marks, low = items
        left_part = tiles[..., :R].astype(jnp.float32)
        right_part = tiles[..., R:].astype(jnp.float32)
        a_up = low[:, :R].astype(jnp.float32)
        a_down = low[:, R:].astype(jnp.float32)
        core = round_half(mult('jbr,jbs->jrs', right_part, k_right) * marks.astype(jnp.float32)[:, None, None])
        mixed_left = round_half(mult('jbr,jrs->jbs', left_part, core))
        first = mult('br,rp->bp', a_up, round_half(mult('br,bp->rp', a_down, omega))) - mult('jbs,jsp->bp', mixed_left, probe)
        first_b = round_half(first)
        second = mult('br,rp->bp', a_down, round_half(mult('br,bp->rp', a_up, first_b))) - mult('jbr,jrp->bp', k_left, round_half(mult('jbs,bp->jsp', mixed_left, first_b)))
        second_b = round_half(second)
        third = mult('br,rp->bp', a_up, round_half(mult('br,bp->rp', a_down, second_b))) - mult('jbs,jsp->bp', mixed_left, round_half(mult('jbr,bp->jrp', k_left, second_b)))
        basis_cols = orthonormal(third)
        basis_b = round_half(basis_cols)
        projected = mult('br,rp->bp', a_down, round_half(mult('br,bp->rp', a_up, basis_b))) - mult('jbr,jrp->bp', k_left, round_half(mult('jbs,bp->jsp', mixed_left, basis_b)))
        return (basis_cols, projected)
    bases, projections = lax.map(one_row, (panel, mask, a_low))
    stacked = jnp.transpose(projections, (1, 0, 2)).reshape(B, TR_TOT * P_SIZE)
    solved = lax.linalg.triangular_solve(factor, stacked, left_side=True, lower=True).reshape(B, TR_TOT, P_SIZE)
    panel_out = jnp.concatenate([bases, jnp.transpose(solved, (1, 0, 2))], axis=2)
    return (panel_out, factor)
```

```python
import functools

import jax
import jax.numpy as jnp
from jax import lax
from jax.experimental import pallas as pl
from jax.experimental.pallas import tpu as pltpu
from jax.sharding import PartitionSpec as P

f32 = jnp.float32
bf16 = jnp.bfloat16

def rcp(p):
    r = pl.reciprocal(p, approx=True)
    return r * (2.0 - p * r)

def strip_eliminate(parts, k0, s):
    first = parts[0]
    lanes = first.shape[1]
    row = lax.broadcasted_iota(jnp.int32, (s, lanes), 0)
    C = [jnp.broadcast_to(first[:, k0 + j:k0 + j + 1], (s, lanes)) for j in range(s)]
    parts = list(parts)
    diag = jnp.ones((s, lanes), f32)
    for j in range(s):
        p = C[j][j:j + 1, :]
        diag = jnp.where(row == j, p, diag)
        if j == s - 1: break
        M = jnp.where(row > j, C[j] * rcp(p), 0.0)
        for k in range(j + 1, s):
            C[k] = C[k] - M * C[k][j:j + 1, :]
        parts = [x - M * x[j:j + 1, :] for x in parts]
    R = lax.rsqrt(diag)
    return [x * R for x in parts]

def tn(a, b, prec=None):
    return lax.dot_general(a, b, (((0,), (0,)), ((), ())), preferred_element_type=f32, precision=prec)

def chol_block(D, n, s, exact=False):
    eye = (lax.broadcasted_iota(jnp.int32, (n, n), 0) == lax.broadcasted_iota(jnp.int32, (n, n), 1)).astype(f32)
    WA, WE = D, eye
    outU, outE = [], []
    for k0 in range(0, n, s):
        a, e = strip_eliminate([WA[:s], WE[:s]], k0, s)
        outU.append(a); outE.append(e)
        if k0 + s < n:
            if exact:
                lhs=a[:, k0 + s:]
                WA = WA[s:] - tn(lhs, a, lax.Precision.HIGHEST)
                WE = WE[s:] - tn(lhs, e, lax.Precision.HIGHEST)
            else:
                ab = a.astype(bf16); eb = e.astype(bf16)
                lhs = ab[:, k0 + s:]
                WA = WA[s:] - tn(lhs, ab)
                WE = WE[s:] - tn(lhs, eb)
    U = jnp.concatenate(outU, 0); E = jnp.concatenate(outE, 0)
    i0=lax.broadcasted_iota(jnp.int32, (n, n), 0); i1=lax.broadcasted_iota(jnp.int32, (n, n), 1)
    U = jnp.where(i1>=i0, U, 0.0)
    return U, E


def diag_kernel(a_ref, b_ref, slab_ref, x_ref, A, Y):
    A[...] = a_ref[...].astype(f32)
    Y[...] = b_ref[...]
    N = a_ref.shape[0]
    nb = N // 128
    for kb in range(nb):
        o = kb * 128
        U, E = chol_block(A[o:o + 128, o:o + 128], 128, 16)
        A[o:o + 128, o:o + 128] = U
        Eb = E.astype(bf16)
        y = jnp.dot(Eb, Y[o:o + 128, :].astype(bf16), preferred_element_type=f32)
        x_ref[o:o + 128, :] = y
        if o + 128 < N:
            panel = jnp.dot(Eb, A[o:o + 128, o + 128:].astype(bf16), preferred_element_type=f32)
            A[o:o + 128, o + 128:] = panel
            pb = panel.astype(bf16)
            for ib in range(kb + 1, nb):
                r = ib * 128
                A[r:r + 128, r:] -= tn(pb[:, r - o - 128:r - o], pb[:, r - o - 128:])
            Y[o + 128:, :] -= tn(pb, y.astype(bf16))
    z = lax.axis_index("rows")
    row = z * 128 + lax.broadcasted_iota(jnp.int32, (128, 128), 0)
    for kb in range(nb):
        o = kb * 128
        block = A[o:o + 128, pl.ds(pl.multiple_of(z * 128, 128), 128)].T
        col = o + lax.broadcasted_iota(jnp.int32, (128, 128), 1)
        slab_ref[:, o:o + 128] = jnp.where(col <= row, block, 0.0)


def factor_and_solve(a, b):
    vm = pl.BlockSpec(memory_space=pltpu.VMEM)
    n = a.shape[0]
    return pl.pallas_call(
        diag_kernel,
        out_shape=(jax.ShapeDtypeStruct((128, n), f32), jax.ShapeDtypeStruct(b.shape, f32)),
        in_specs=[vm] * 2,
        out_specs=[vm] * 2,
        scratch_shapes=[pltpu.VMEM(a.shape, f32), pltpu.VMEM(b.shape, f32)],
        compiler_params=pltpu.CompilerParams(vmem_limit_bytes=48 * 2**20),
        name="diag",
    )(a, b)


def gram_kernel(g_ref, c_ref):
    for i in range(g_ref.shape[0]):
        c_ref[i] = chol_block(g_ref[i], 64, 16, exact=True)[1]


def inverse_factors(grams):
    vm = pl.BlockSpec(memory_space=pltpu.VMEM)
    return pl.pallas_call(
        gram_kernel,
        out_shape=jax.ShapeDtypeStruct(grams.shape, f32),
        in_specs=[vm],
        out_specs=vm,
        name="gram",
    )(grams)

def joined_along(blocks, dim):
    blocks = jnp.moveaxis(blocks, 0, dim)
    lengths = blocks.shape
    return blocks.reshape(*lengths[:dim], lengths[dim] * lengths[dim + 1], *lengths[dim + 2 :])


def from_everyone(value, axis):
    count = lax.axis_size(axis)
    return lax.all_to_all(
        jnp.broadcast_to(value[None], (count, *value.shape)), axis, 0, 0, tiled=True
    )


def collect(value, axis, dim):
    return joined_along(from_everyone(value, axis), dim)


def split_up(value, dim, count):
    before, after = (value.shape[:dim], value.shape[dim + 1 :])
    return jnp.moveaxis(value.reshape(*before, count, -1, *after), dim, 0)


def sum_at_owner(value, axis, dim):
    count = lax.axis_size(axis)
    blocks = lax.all_to_all(split_up(value, dim, count), axis, 0, 0, tiled=True)
    return jnp.sum(blocks.astype(jnp.float32), axis=0)


def padded_to(lines, count):
    spare = -lines.shape[0] % count
    if not spare:
        return lines
    return jnp.concatenate([lines, jnp.zeros((spare, *lines.shape[1:]), lines.dtype)])


def total_of(value, axes):
    lines = value.reshape(-1, value.shape[-1])
    own = sum_at_owner(padded_to(lines, lax.axis_size(axes)), axes, 0)
    whole = collect(own.astype(jnp.bfloat16), axes, 0)
    return whole[: len(lines)].reshape(value.shape).astype(jnp.float32)


def summed_on_arrival(value, axis, dim):
    count = lax.axis_size(axis)
    blocks = lax.all_to_all(split_up(value, dim, count), axis, 0, 0, tiled=True)
    return jnp.sum(blocks, axis=0)


def apply_inverse(gram_matrix, field):
    inverse = inverse_factors(gram_matrix)
    return jnp.einsum("bip,iqp->biq", field, inverse, precision=lax.Precision.HIGHEST)


def shards(panel, row_k, mask, a_low, a_diag, sketch):
    f32 = jnp.float32
    bf16 = jnp.bfloat16
    half_width = panel.shape[-1] // 2
    tile_order = panel.shape[2]
    rows_here = panel.shape[0]
    rank_cols = sketch.shape[1]
    share_count = tile_order // lax.axis_size("cols")
    share_offset = lax.axis_index("cols") * share_count

    def flatten_rows(values):
        return values.reshape(values.shape[0], rows_here * rank_cols)

    def split_rows(values):
        return values.reshape(values.shape[0], rows_here, rank_cols)

    whole_row = collect(row_k, "rows", 1)
    k_left = whole_row[..., :half_width]
    k_right = whole_row[..., half_width:]
    own_left = row_k[..., :half_width]
    diag_core = jnp.einsum("jbr,jbs->jrs", k_right, k_right, preferred_element_type=f32).astype(
        bf16
    )
    own_mixed = jnp.einsum("jbr,jrs->jbs", own_left, diag_core, preferred_element_type=f32).astype(
        bf16
    )
    diag_part = jnp.einsum("jbs,jcs->bc", own_mixed, k_left, preferred_element_type=f32)
    diag_sum = total_of(diag_part.astype(jnp.bfloat16), "cols")
    whole_diag = lax.all_gather(
        (a_diag - diag_sum).astype(jnp.bfloat16), "rows", axis=0, tiled=True
    )
    left_part = panel[..., :half_width]
    right_part = panel[..., half_width:]
    weights = mask.astype(f32)[:, :, None, None]
    core = (
        jnp.einsum("ijbr,jbs->ijrs", right_part, k_right, preferred_element_type=f32) * weights
    ).astype(bf16)
    mixed_left = jnp.einsum("ijbr,ijrs->ijbs", left_part, core, preferred_element_type=f32).astype(
        bf16
    )
    probe_core = jnp.einsum("jbr,bp->jrp", k_left, sketch, preferred_element_type=f32).astype(bf16)
    a_up = a_low[..., :half_width]
    a_down = a_low[..., half_width:]

    def low_term(outer, inner, field):
        inner_core = jnp.einsum("ibr,bip->irp", inner, field, preferred_element_type=f32).astype(
            bf16
        )
        return jnp.einsum("ibr,irp->bip", outer, inner_core, preferred_element_type=f32)

    inner_first = jnp.einsum("ibr,bp->irp", a_down, sketch, preferred_element_type=f32).astype(bf16)
    a_first = jnp.einsum("ibr,irp->bip", a_up, inner_first, preferred_element_type=f32)
    piece = mixed_left
    terms = jnp.einsum("ijbs,jsp->bip", piece, probe_core, preferred_element_type=f32)
    first_share = summed_on_arrival(
        terms.reshape(share_count * lax.axis_size("cols"), rows_here * rank_cols), "cols", 0
    )
    own_first = (
        lax.dynamic_slice_in_dim(flatten_rows(a_first), share_offset, share_count, 0) - first_share
    )
    first_b = split_rows(collect(own_first.astype(bf16), "cols", 0))
    back_core = jnp.einsum(
        "ijbs,bip->ijsp", mixed_left, first_b, preferred_element_type=f32
    ).astype(bf16)
    a_second = low_term(a_down, a_up, first_b)
    piece = k_left
    terms = jnp.einsum("jbr,ijrp->bip", piece, back_core, preferred_element_type=f32)
    second_share = summed_on_arrival(
        terms.reshape(share_count * lax.axis_size("cols"), rows_here * rank_cols), "cols", 0
    )
    own_second = (
        lax.dynamic_slice_in_dim(flatten_rows(a_second), share_offset, share_count, 0)
        - second_share
    )
    second_b = split_rows(collect(own_second.astype(bf16), "cols", 0))
    fore_core = jnp.einsum("jbr,bip->ijrp", k_left, second_b, preferred_element_type=f32).astype(
        bf16
    )
    third_terms = jnp.einsum("ijbs,ijsp->bip", mixed_left, fore_core, preferred_element_type=f32)
    a_third = low_term(a_up, a_down, second_b)
    third = a_third - split_rows(total_of(flatten_rows(third_terms).astype(jnp.bfloat16), "cols"))
    gram_matrix = jnp.einsum("bip,biq->ipq", third, third, precision=lax.Precision.HIGHEST)
    basis_cols = apply_inverse(gram_matrix, third)
    basis_b = basis_cols.astype(bf16)
    last_core = jnp.einsum(
        "ijbs,bip->ijsp", mixed_left, basis_b, preferred_element_type=f32
    ).astype(bf16)
    last_terms = jnp.einsum("jbr,ijrp->bip", k_left, last_core, preferred_element_type=f32)
    projected = low_term(a_down, a_up, basis_b) - split_rows(
        total_of(flatten_rows(last_terms).astype(jnp.bfloat16), "cols")
    )
    diag_out, solved = factor_and_solve(whole_diag, flatten_rows(projected))
    solved = split_rows(solved)
    panel_out = jnp.concatenate(
        [jnp.transpose(basis_cols, (1, 0, 2)), jnp.transpose(solved, (1, 0, 2))], axis=2
    )
    return (panel_out, diag_out)


def solution(mesh):
    return jax.shard_map(
        shards,
        mesh=mesh,
        in_specs=(
            P("rows", "cols", None, None),
            P("cols", "rows", None),
            P("rows", "cols"),
            P("rows", None, None),
            P("rows", None),
            P(),
        ),
        out_specs=(P("rows", None, None), P("rows", None)),
        check_vma=False,
    )
```

```python
import functools

import jax
import jax.numpy as jnp
from jax import lax
from jax.experimental import pallas as pl
from jax.experimental.pallas import tpu as pltpu
from jax.sharding import PartitionSpec as P

f32 = jnp.float32
bf16 = jnp.bfloat16
MESH = pl.DeviceIdType.MESH
HIGHEST = lax.Precision.HIGHEST

def rcp(p):
    r = pl.reciprocal(p, approx=True)
    return r * (2.0 - p * r)

def strip_eliminate(parts, k0, s):
    first = parts[0]
    lanes = first.shape[1]
    row = lax.broadcasted_iota(jnp.int32, (s, lanes), 0)
    C = [jnp.broadcast_to(first[:, k0 + j:k0 + j + 1], (s, lanes)) for j in range(s)]
    parts = list(parts)
    diag = jnp.ones((s, lanes), f32)
    for j in range(s):
        p = C[j][j:j + 1, :]
        diag = jnp.where(row == j, p, diag)
        if j == s - 1: break
        M = jnp.where(row > j, C[j] * rcp(p), 0.0)
        for k in range(j + 1, s):
            C[k] = C[k] - M * C[k][j:j + 1, :]
        parts = [x - M * x[j:j + 1, :] for x in parts]
    R = lax.rsqrt(diag)
    return [x * R for x in parts]

def tn(a, b, prec=None):
    return lax.dot_general(a, b, (((0,), (0,)), ((), ())), preferred_element_type=f32, precision=prec)

def chol_block(D, n, s, exact=False):
    eye = (lax.broadcasted_iota(jnp.int32, (n, n), 0) == lax.broadcasted_iota(jnp.int32, (n, n), 1)).astype(f32)
    WA, WE = D, eye
    outU, outE = [], []
    for k0 in range(0, n, s):
        a, e = strip_eliminate([WA[:s], WE[:s]], k0, s)
        outU.append(a); outE.append(e)
        if k0 + s < n:
            if exact:
                lhs=a[:, k0 + s:]
                WA = WA[s:] - tn(lhs, a, lax.Precision.HIGHEST)
                WE = WE[s:] - tn(lhs, e, lax.Precision.HIGHEST)
            else:
                ab = a.astype(bf16); eb = e.astype(bf16)
                lhs = ab[:, k0 + s:]
                WA = WA[s:] - tn(lhs, ab)
                WE = WE[s:] - tn(lhs, eb)
    U = jnp.concatenate(outU, 0); E = jnp.concatenate(outE, 0)
    i0=lax.broadcasted_iota(jnp.int32, (n, n), 0); i1=lax.broadcasted_iota(jnp.int32, (n, n), 1)
    U = jnp.where(i1>=i0, U, 0.0)
    return U, E


def inverse_pair(gram):
    n, s = 64, 16
    low = lax.broadcasted_iota(jnp.int32, (s, 128), 1) < n
    row = lax.broadcasted_iota(jnp.int32, (s, 128), 0)
    lanes = lax.broadcasted_iota(jnp.int32, (n, 128), 1)
    left = lanes < n
    A = jnp.where(left, gram[:n], gram[n:])
    E = (lax.rem(lanes, n) == lax.broadcasted_iota(jnp.int32, (n, 128), 0)).astype(f32)
    done = []
    for k0 in range(0, n, s):
        a, e = A[:s], E[:s]
        C = [
            jnp.where(
                low,
                jnp.broadcast_to(a[:, k0 + j:k0 + j + 1], (s, 128)),
                jnp.broadcast_to(a[:, n + k0 + j:n + k0 + j + 1], (s, 128)),
            )
            for j in range(s)
        ]
        diag = jnp.ones((s, 128), f32)
        for j in range(s):
            p = C[j][j:j + 1, :]
            diag = jnp.where(row == j, p, diag)
            if j == s - 1:
                break
            r = rcp(p)
            r = r * (2.0 - p * r)
            M = jnp.where(row > j, C[j] * r, 0.0)
            for k in range(j + 1, s):
                C[k] = C[k] - M * C[k][j:j + 1, :]
            a = a - M * a[j:j + 1, :]
            e = e - M * e[j:j + 1, :]
        R = lax.rsqrt(diag)
        a, e = a * R, e * R
        done.append(e)
        if k0 + s < n:
            both = tn(a, jnp.concatenate([a, e], axis=1), HIGHEST)
            both = [both[:, :128], both[:, 128:]]
            keep = left[k0 + s:]
            step = [jnp.where(keep, x[k0 + s:n], x[n + k0 + s:]) for x in both]
            A, E = A[s:] - step[0], E[s:] - step[1]
    E = jnp.concatenate(done, axis=0)
    return jnp.concatenate([jnp.where(left, E, 0.0), jnp.where(left, 0.0, E)], axis=0)


def nn(a, b, prec=None):
    return jnp.dot(a, b, preferred_element_type=f32, precision=prec)


def nt(a, b, prec=None):
    return lax.dot_general(a, b, (((1,), (1,)), ((), ())), preferred_element_type=f32, precision=prec)


def low_lanes(n):
    return lax.broadcasted_iota(jnp.int32, (n, 128), 1) < 64


def sketch_kernel(
    panel, row_k, mask, a_low, a_diag, sketch,
    basis_ref, proj_ref, full,
    ROW, LT, ACC, MIX, S2, DP, DRS, FULL, TS, RS, FB, SB, TH, PB,
    zsend, zrecv, dsend, drecv, csend, crecv, rsend, rrecv, asend, arecv,
    *, NC, NR,
):
    B = NR * 128
    share = B // NC
    strips = 8
    wide = B // (NC // strips)
    c = lax.axis_index("cols")
    z = lax.axis_index("rows")
    base = pl.multiple_of(c * share, share)
    barrier = pltpu.get_barrier_semaphore()

    def col_of(d):
        return lax.rem(c + d, NC)

    def row_of(d):
        return lax.rem(z + d + NR, NR)

    def each(n, body):
        def step(d, carry):
            body(d)
            return carry
        lax.fori_loop(1, n, step, 0)

    each(NC, lambda d: pl.semaphore_signal(barrier, 1, device_id={"cols": col_of(d)}, device_id_type=MESH))
    each(NR, lambda d: pl.semaphore_signal(barrier, 1, device_id={"rows": row_of(d)}, device_id_type=MESH))

    S2[...] = jnp.concatenate([sketch[...], sketch[...]], axis=1)
    for i in range(2):
        LT[384 + 128 * i:512 + 128 * i, :] = a_low[i].T
    for j in range(3):
        ROW[j, pl.ds(pl.multiple_of(z * 128, 128), 128), :] = row_k[j]
        ACC[j] = jnp.zeros_like(ACC[j])
    pl.semaphore_wait(barrier, NC + NR - 2)

    def slab(owner):
        return pl.ds(pl.multiple_of(owner * 128, 128), 128)

    def hop(way, step, owner):
        place = ROW.at[:, slab(owner), :]
        return pltpu.make_async_remote_copy(
            src_ref=place, dst_ref=place,
            send_sem=zsend.at[way, step], recv_sem=zrecv.at[way, step],
            device_id={"rows": row_of(1 if way == 0 else -1)}, device_id_type=MESH,
        )

    def absorb(owner):
        for j in range(3):
            r = ROW[j, slab(owner), :]
            rt = r.T
            LT[640 + 128 * j:768 + 128 * j, slab(owner)] = rt
            right = jnp.concatenate(
                [panel[0, j, slab(owner), :], panel[1, j, slab(owner), :], r, S2[slab(owner), :]], axis=1
            )
            ACC[j] += nn(rt, right)

    ups, downs = NR // 2, NR - 1 - NR // 2
    hops = [hop(0, 0, z)] + ([hop(1, 0, z)] if downs else [])
    for h in hops:
        h.start()
    absorb(z)
    for s in range(ups):
        arrived = [row_of(-1 - s)]
        hop(0, s, arrived[0]).wait_recv()
        if s + 1 < ups:
            h = hop(0, s + 1, arrived[0])
            h.start()
            hops.append(h)
        if s < downs:
            arrived.append(row_of(1 + s))
            hop(1, s, arrived[1]).wait_recv()
            if s + 1 < downs:
                h = hop(1, s + 1, arrived[1])
                h.start()
                hops.append(h)
        for owner in arrived:
            absorb(owner)

    part = jnp.zeros((128, B), f32)
    for j in range(3):
        core = pltpu.roll(ACC[j, 64:128, 256:384], 64, 1)
        core = jnp.where(low_lanes(64), core, 0.0).astype(bf16)
        core = jnp.concatenate([core, jnp.zeros((64, 128), bf16)], axis=0)
        own = nn(ROW[j, slab(z), :], core).astype(bf16)
        part = part + nn(own, LT[640 + 128 * j:768 + 128 * j, :])
    DP[...] = part.astype(bf16)

    def piece(owner):
        return (
            pl.ds(pl.multiple_of(lax.rem(owner, strips) * 16, 16), 16),
            pl.ds(pl.multiple_of(lax.div(owner, strips) * wide, 128), wide),
        )

    def send_diag(d):
        rows, columns = piece(col_of(d))
        pltpu.make_async_remote_copy(
            src_ref=DP.at[rows, columns], dst_ref=DRS.at[d - 1],
            send_sem=dsend.at[0], recv_sem=drecv.at[0],
            device_id={"cols": col_of(d)}, device_id_type=MESH,
        ).start()

    def all_in(ref, sem):
        pltpu.make_async_copy(ref, ref, sem).wait()

    each(NC, send_diag)

    weight = []
    for i in range(2):
        for j in range(3):
            block = ACC[j, :, 128 * i:128 * i + 128] * mask[i, j].astype(f32)
            flat = jnp.where(low_lanes(64), pltpu.roll(block[64:, :], 64, 1), 0.0).astype(bf16)
            m = 3 * i + j
            turned = block.T[64:, :]
            if m % 2 == 0:
                turned = jnp.where(low_lanes(64), pltpu.roll(turned, 64, 1), 0.0)
            else:
                turned = jnp.where(low_lanes(64), 0.0, turned)
            weight.append(jnp.concatenate([turned.astype(bf16), jnp.zeros((64, 128), bf16)], axis=0))
            LT[64 * m:64 * m + 64, :] = nt(flat, panel[i, j]).astype(bf16)
    for t in range(3):
        m, n = 2 * t, 2 * t + 1
        MIX[:, 128 * t:128 * t + 128] = (
            nn(panel[m // 3, m % 3], weight[m]) + nn(panel[n // 3, n % 3], weight[n])
        ).astype(bf16)

    def spread(inner):
        keep = low_lanes(192)
        zero = jnp.zeros_like(inner)
        return jnp.concatenate([jnp.where(keep, inner, zero), jnp.where(keep, zero, inner)], axis=0)

    def start_sum(n, terms):
        TS[n] = terms
        def send(d):
            pltpu.make_async_remote_copy(
                src_ref=TS.at[n, pl.ds(pl.multiple_of(col_of(d) * share, share), share), :],
                dst_ref=RS.at[n, d - 1],
                send_sem=rsend.at[n], recv_sem=rrecv.at[n],
                device_id={"cols": col_of(d)}, device_id_type=MESH,
            ).start()
        each(NC, send)

    def end_sum(n):
        all_in(RS.at[n], rrecv.at[n])
        return TS[n, pl.ds(base, share), :] + jnp.sum(RS[n], axis=0)

    def start_gather(n, whole, own):
        place = whole.at[pl.ds(base, share), :]
        place[...] = own
        def send(d):
            pltpu.make_async_remote_copy(
                src_ref=place, dst_ref=place, send_sem=asend.at[n], recv_sem=arecv.at[n],
                device_id={"cols": col_of(d)}, device_id_type=MESH,
            ).start()
        each(NC, send)

    def end_gather(n, whole):
        all_in(whole.at[pl.ds(0, B - share), :], arecv.at[n])

    def low_share(inner, up):
        total = jnp.zeros((share, 128), f32)
        zero = jnp.zeros((64, 128), bf16)
        for i in range(2):
            half = inner[128 * i + 64:128 * i + 128] if up else inner[128 * i:128 * i + 64]
            keep = low_lanes(64) if i == 0 else jnp.logical_not(low_lanes(64))
            half = jnp.where(keep, half, 0.0).astype(bf16)
            right = jnp.concatenate([half, zero] if up else [zero, half], axis=0)
            total = total + nn(a_low[i, pl.ds(base, share), :], right)
        return total

    def back_terms(back):
        zero = jnp.zeros((64, 128), bf16)
        total = jnp.zeros((B, 128), f32)
        for j in range(3):
            mine = jnp.where(low_lanes(64), back[64 * j:64 * j + 64], back[192 + 64 * j:256 + 64 * j])
            total = total + nn(ROW[j], jnp.concatenate([mine.astype(bf16), zero], axis=0))
        return total

    probe = jnp.concatenate([ACC[j, :64, 384:512] for j in range(3)], axis=0)
    start_sum(0, nn(MIX[...], spread(probe).astype(bf16)))
    low = low_share(nn(LT[384:640, :], S2[...]), True)
    all_in(DRS, drecv.at[0])
    rows, columns = piece(c)
    own = a_diag[rows, columns] - (
        DP[rows, columns].astype(f32) + jnp.sum(DRS[...].astype(f32), axis=0)
    )
    strip = lax.rem(c, strips)
    pair, core = lax.div(strip, 2), lax.rem(strip, 2)
    FULL[z, pair, core, :, columns] = own.astype(bf16)

    def send_rows(d):
        place = FULL.at[z, pair, core, :, columns]
        pltpu.make_async_remote_copy(
            src_ref=place, dst_ref=place, send_sem=dsend.at[1], recv_sem=drecv.at[1],
            device_id={"rows": row_of(d)}, device_id_type=MESH,
        ).start()

    each(NR, send_rows)
    start_gather(0, FB, (low - end_sum(0)).astype(bf16))
    all_in(FULL.at[pl.ds(0, NR - 1), pair, core, :, columns], drecv.at[1])
    end_gather(0, FB)

    inner = nn(LT[:640, :], FB[...])
    start_sum(1, back_terms(inner[:384]))

    def to_chip(d):
        place = FULL.at[:, pair, core, :, columns]
        return pltpu.make_async_remote_copy(
            src_ref=place, dst_ref=place, send_sem=csend.at[d - 1], recv_sem=crecv.at[d - 1],
            device_id={"cols": lax.rem(c + 2 * d, NC)}, device_id_type=MESH,
        )

    each(NC // 2, lambda d: to_chip(d).start())
    low = low_share(inner[384:], False)
    start_gather(1, SB, (low - end_sum(1)).astype(bf16))
    end_gather(1, SB)

    inner = nn(LT[384:, :], SB[...])
    fore = jnp.concatenate([inner[256 + 128 * j:320 + 128 * j] for j in range(3)], axis=0)
    start_sum(2, nn(MIX[...], spread(fore).astype(bf16)))
    low = low_share(inner[:256], True)
    each(NC // 2, lambda d: to_chip(d).wait_recv())
    place = FULL.at[:, :, core]
    to_core = pltpu.make_async_remote_copy(
        src_ref=place, dst_ref=place, send_sem=dsend.at[2], recv_sem=drecv.at[2],
        device_id={"cols": c + 1 - 2 * core}, device_id_type=MESH,
    )
    to_core.start()
    start_gather(2, TH, low - end_sum(2))
    end_gather(2, TH)

    third = TH[...]
    basis = nt(third, inverse_pair(nn(third.T, third, HIGHEST)), HIGHEST)
    basis_ref[...] = basis

    inner = nn(LT[:640, :], basis.astype(bf16))
    start_sum(3, back_terms(inner[:384]))
    low = low_share(inner[384:], False)
    start_gather(3, PB, (low - end_sum(3)).astype(bf16))
    to_core.wait_recv()
    full[...] = FULL[...]
    end_gather(3, PB)
    proj_ref[...] = PB[...]

    for h in hops:
        h.wait_send()
    all_in(DRS, dsend.at[0])
    all_in(FULL.at[pl.ds(0, NR - 1), pair, core, :, columns], dsend.at[1])
    each(NC // 2, lambda d: to_chip(d).wait_send())
    to_core.wait_send()
    for n in range(4):
        all_in(RS.at[n], rsend.at[n])
    for n, whole in enumerate((FB, SB, TH, PB)):
        all_in(whole.at[pl.ds(0, B - share), :], asend.at[n])


def sketch_sums(panel, row_k, mask, a_low, a_diag, sketch):
    NC, NR = lax.axis_size("cols"), lax.axis_size("rows")
    B = NR * 128
    share = B // NC
    wide = B // (NC // 8)
    vm = pl.BlockSpec(memory_space=pltpu.VMEM)
    dma = pltpu.SemaphoreType.DMA
    shape = jax.ShapeDtypeStruct
    return pl.pallas_call(
        functools.partial(sketch_kernel, NC=NC, NR=NR),
        out_shape=(
            shape((B, 128), f32), shape((B, 128), bf16), shape((NR, 4, 2, 16, B), bf16),
        ),
        in_specs=[vm, vm, pl.BlockSpec(memory_space=pltpu.SMEM), vm, vm, vm],
        out_specs=[vm] * 3,
        scratch_shapes=[
            pltpu.VMEM((3, B, 128), bf16),
            pltpu.VMEM((1024, B), bf16),
            pltpu.VMEM((3, 128, 512), f32),
            pltpu.VMEM((B, 384), bf16),
            pltpu.VMEM((B, 128), bf16),
            pltpu.VMEM((128, B), bf16),
            pltpu.VMEM((NC - 1, 16, wide), bf16),
            pltpu.VMEM((NR, 4, 2, 16, B), bf16),
            pltpu.VMEM((4, B, 128), f32),
            pltpu.VMEM((4, NC - 1, share, 128), f32),
            pltpu.VMEM((B, 128), bf16),
            pltpu.VMEM((B, 128), bf16),
            pltpu.VMEM((B, 128), f32),
            pltpu.VMEM((B, 128), bf16),
            dma((2, 4)), dma((2, 4)), dma((3,)), dma((3,)),
            dma((NC // 2,)), dma((NC // 2,)),
            dma((4,)), dma((4,)), dma((4,)), dma((4,)),
        ],
        compiler_params=pltpu.CompilerParams(
            collective_id=0, has_side_effects=True, vmem_limit_bytes=50 * 2**20
        ),
        name="sketches",
    )(panel, row_k, mask, a_low, a_diag, sketch)


def diag_kernel(a_ref, proj_ref, basis_ref, panel_ref, slab_ref, A, Y):
    A[...] = a_ref[...].astype(f32)
    Y[...] = proj_ref[...].astype(f32)
    N = a_ref.shape[0]
    nb = N // 128
    left = lax.broadcasted_iota(jnp.int32, (128, 128), 1) < 64
    for kb in range(nb):
        o = kb * 128
        U, E = chol_block(A[o:o + 128, o:o + 128], 128, 16)
        A[o:o + 128, o:o + 128] = U
        Eb = E.astype(bf16)
        y = nn(Eb, Y[o:o + 128, :].astype(bf16))
        basis = basis_ref[o:o + 128, :]
        panel_ref[0, o:o + 128, :] = jnp.where(left, basis, pltpu.roll(y, 64, 1))
        panel_ref[1, o:o + 128, :] = jnp.where(left, pltpu.roll(basis, 64, 1), y)
        if o + 128 < N:
            panel = nn(Eb, A[o:o + 128, o + 128:].astype(bf16))
            A[o:o + 128, o + 128:] = panel
            pb = panel.astype(bf16)
            for ib in range(kb + 1, nb):
                r = ib * 128
                A[r:r + 128, r:] -= tn(pb[:, r - o - 128:r - o], pb[:, r - o - 128:])
            Y[o + 128:, :] -= tn(pb, y.astype(bf16))
    z = lax.axis_index("rows")
    row = z * 128 + lax.broadcasted_iota(jnp.int32, (128, 128), 0)
    for kb in range(nb):
        o = kb * 128
        block = A[o:o + 128, pl.ds(pl.multiple_of(z * 128, 128), 128)].T
        col = o + lax.broadcasted_iota(jnp.int32, (128, 128), 1)
        slab_ref[:, o:o + 128] = jnp.where(col <= row, block, 0.0)


def factor_and_solve(a, proj, basis):
    vm = pl.BlockSpec(memory_space=pltpu.VMEM)
    n = a.shape[0]
    return pl.pallas_call(
        diag_kernel,
        out_shape=(jax.ShapeDtypeStruct((2, n, 128), f32), jax.ShapeDtypeStruct((128, n), f32)),
        in_specs=[vm] * 3,
        out_specs=[vm] * 2,
        scratch_shapes=[pltpu.VMEM(a.shape, f32), pltpu.VMEM((n, 128), f32)],
        compiler_params=pltpu.CompilerParams(vmem_limit_bytes=48 * 2**20),
        name="diag",
    )(a, proj, basis)


def shards(panel, row_k, mask, a_low, a_diag, sketch):
    basis, proj, full = sketch_sums(panel, row_k, mask, a_low, a_diag, sketch)
    n = basis.shape[0]
    return factor_and_solve(full.reshape(n, n), proj, basis)


def solution(mesh):
    return jax.shard_map(
        shards,
        mesh=mesh,
        in_specs=(
            P("rows", "cols", None, None),
            P("cols", "rows", None),
            P("rows", "cols"),
            P("rows", None, None),
            P("rows", None),
            P(),
        ),
        out_specs=(P("rows", None, None), P("rows", None)),
        check_vma=False,
    )
```

```python
import functools

import jax
import jax.numpy as jnp
from jax import lax
from jax.experimental import pallas as pl
from jax.experimental.pallas import tpu as pltpu
from jax.sharding import PartitionSpec as P

f32 = jnp.float32
bf16 = jnp.bfloat16
MESH = pl.DeviceIdType.MESH
HIGHEST = lax.Precision.HIGHEST

def rcp(p):
    r = pl.reciprocal(p, approx=True)
    return r * (2.0 - p * r)

def strip_eliminate(parts, k0, s):
    first = parts[0]
    lanes = first.shape[1]
    row = lax.broadcasted_iota(jnp.int32, (s, lanes), 0)
    C = [jnp.broadcast_to(first[:, k0 + j:k0 + j + 1], (s, lanes)) for j in range(s)]
    parts = list(parts)
    diag = jnp.ones((s, lanes), f32)
    for j in range(s):
        p = C[j][j:j + 1, :]
        diag = jnp.where(row == j, p, diag)
        if j == s - 1: break
        M = jnp.where(row > j, C[j] * rcp(p), 0.0)
        for k in range(j + 1, s):
            C[k] = C[k] - M * C[k][j:j + 1, :]
        parts = [x - M * x[j:j + 1, :] for x in parts]
    R = lax.rsqrt(diag)
    return [x * R for x in parts]

def tn(a, b, prec=None):
    return lax.dot_general(a, b, (((0,), (0,)), ((), ())), preferred_element_type=f32, precision=prec)

def chol_block(D, n, s):
    eye = (lax.broadcasted_iota(jnp.int32, (n, n), 0) == lax.broadcasted_iota(jnp.int32, (n, n), 1)).astype(f32)
    WA, WE = D, eye
    outU, outE = [], []
    for k0 in range(0, n, s):
        a, e = strip_eliminate([WA[:s], WE[:s]], k0, s)
        outU.append(a)
        outE.append(e)
        if k0 + s < n:
            ab = a.astype(bf16)
            eb = e.astype(bf16)
            lhs = ab[:, k0 + s:]
            WA = WA[s:] - tn(lhs, ab)
            WE = WE[s:] - tn(lhs, eb)
            yield
    U = jnp.concatenate(outU, 0)
    E = jnp.concatenate(outE, 0)
    i0 = lax.broadcasted_iota(jnp.int32, (n, n), 0)
    i1 = lax.broadcasted_iota(jnp.int32, (n, n), 1)
    return jnp.where(i1 >= i0, U, 0.0), E


def together(*works):
    given = [None] * len(works)
    live = list(range(len(works)))
    while live:
        for n in list(live):
            try:
                next(works[n])
            except StopIteration as stop:
                given[n] = stop.value
                live.remove(n)
    return given


def inverse_pair(gram):
    n, s = 64, 16
    low = lax.broadcasted_iota(jnp.int32, (s, 128), 1) < n
    row = lax.broadcasted_iota(jnp.int32, (s, 128), 0)
    lanes = lax.broadcasted_iota(jnp.int32, (n, 128), 1)
    left = lanes < n
    A = jnp.where(left, gram[:n], gram[n:])
    E = (lax.rem(lanes, n) == lax.broadcasted_iota(jnp.int32, (n, 128), 0)).astype(f32)
    done = []
    for k0 in range(0, n, s):
        a, e = A[:s], E[:s]
        C = [
            jnp.where(
                low,
                jnp.broadcast_to(a[:, k0 + j:k0 + j + 1], (s, 128)),
                jnp.broadcast_to(a[:, n + k0 + j:n + k0 + j + 1], (s, 128)),
            )
            for j in range(s)
        ]
        diag = jnp.ones((s, 128), f32)
        for j in range(s):
            p = C[j][j:j + 1, :]
            diag = jnp.where(row == j, p, diag)
            if j == s - 1:
                break
            r = rcp(p)
            r = r * (2.0 - p * r)
            M = jnp.where(row > j, C[j] * r, 0.0)
            for k in range(j + 1, s):
                C[k] = C[k] - M * C[k][j:j + 1, :]
            a = a - M * a[j:j + 1, :]
            e = e - M * e[j:j + 1, :]
        R = lax.rsqrt(diag)
        a, e = a * R, e * R
        done.append(e)
        if k0 + s < n:
            both = tn(a, jnp.concatenate([a, e], axis=1), HIGHEST)
            both = [both[:, :128], both[:, 128:]]
            keep = left[k0 + s:]
            step = [jnp.where(keep, x[k0 + s:n], x[n + k0 + s:]) for x in both]
            A, E = A[s:] - step[0], E[s:] - step[1]
            yield
    E = jnp.concatenate(done, axis=0)
    return jnp.concatenate([jnp.where(left, E, 0.0), jnp.where(left, 0.0, E)], axis=0)


def nn(a, b, prec=None):
    return jnp.dot(a, b, preferred_element_type=f32, precision=prec)


def nt(a, b, prec=None):
    return lax.dot_general(a, b, (((1,), (1,)), ((), ())), preferred_element_type=f32, precision=prec)


def low_lanes(n):
    return lax.broadcasted_iota(jnp.int32, (n, 128), 1) < 64


def panel_kernel(
    panel_in, row_in, mask, low_in, diag_in, sketch,
    panel_ref, slab_ref,
    panel, a_low, a_diag, ROW, LT, ACC, MIX, S2, DP, DRS, FULL, TS, XS, YS, RS, FB, SB, TH, PB, BS,
    A, LOW, INV, Y,
    lsem, zsend, zrecv, dsend, drecv, csend, crecv, xsend, xrecv, rsend, rrecv, asend, arecv, bsend, brecv,
    *, NC, NR,
):
    B = NR * 128
    share = B // NC
    half = NC // 2
    strips = 8
    wide = B // (NC // strips)
    c = lax.axis_index("cols")
    z = lax.axis_index("rows")
    core, chip = lax.rem(c, 2), lax.div(c, 2)
    other = {"cols": c + 1 - 2 * core}
    barrier = pltpu.get_barrier_semaphore()

    def col_of(d):
        return lax.rem(c + d, NC)

    def chip_of(d):
        return lax.rem(chip + d, half)

    def row_of(d):
        return lax.rem(z + d + NR, NR)

    def slab(owner):
        return pl.ds(pl.multiple_of(owner * 128, 128), 128)

    def each(n, body):
        def step(d, carry):
            body(d)
            return carry
        lax.fori_loop(1, n, step, 0)

    loads = [
        pltpu.make_async_copy(row_in, ROW.at[:, slab(z), :], lsem.at[0]),
        pltpu.make_async_copy(panel_in, panel, lsem.at[1]),
        pltpu.make_async_copy(low_in, a_low, lsem.at[2]),
        pltpu.make_async_copy(diag_in, a_diag, lsem.at[3]),
    ]
    for load in loads:
        load.start()
    each(NC, lambda d: pl.semaphore_signal(barrier, 1, device_id={"cols": col_of(d)}, device_id_type=MESH))
    each(NR, lambda d: pl.semaphore_signal(barrier, 1, device_id={"rows": row_of(d)}, device_id_type=MESH))
    S2[...] = jnp.concatenate([sketch[...], sketch[...]], axis=1)
    for j in range(3):
        ACC[j] = jnp.zeros_like(ACC[j])
    loads[0].wait()
    pl.semaphore_wait(barrier, NC + NR - 2)

    def hop(way, step, j, owner):
        place = ROW.at[j, slab(owner), :]
        return pltpu.make_async_remote_copy(
            src_ref=place, dst_ref=place,
            send_sem=zsend.at[way, step, j], recv_sem=zrecv.at[way, step, j],
            device_id={"rows": row_of(1 if way == 0 else -1)}, device_id_type=MESH,
        )

    def absorb(owner, j):
        r = ROW[j, slab(owner), :]
        rt = r.T
        LT[640 + 128 * j:768 + 128 * j, slab(owner)] = rt
        right = jnp.concatenate(
            [panel[0, j, slab(owner), :], panel[1, j, slab(owner), :], r, S2[slab(owner), :]], axis=1
        )
        ACC[j] += nn(rt, right)

    last = NR // 2 - 1

    def passes(way, step, j):
        return step < last or (step == last and (way == 0) == (j < 2))

    hops = []
    for j in range(3):
        for way in range(2):
            if passes(way, 0, j):
                hops.append(hop(way, 0, j, z))
                hops[-1].start()
    loads[1].wait()
    for j in range(3):
        absorb(z, j)
    loads[2].wait()
    for i in range(2):
        LT[384 + 128 * i:512 + 128 * i, :] = a_low[i].T
    for s in range(last + 1):
        came = []
        for j in range(3):
            for way in range(2):
                if not passes(way, s, j):
                    continue
                owner = row_of(-1 - s if way == 0 else 1 + s)
                hop(way, s, j, owner).wait_recv()
                if passes(way, s + 1, j):
                    hops.append(hop(way, s + 1, j, owner))
                    hops[-1].start()
                came.append((owner, j))
        for owner, j in came:
            absorb(owner, j)

    part = jnp.zeros((128, B), f32)
    for j in range(3):
        square = pltpu.roll(ACC[j, 64:128, 256:384], 64, 1)
        square = jnp.where(low_lanes(64), square, 0.0).astype(bf16)
        square = jnp.concatenate([square, jnp.zeros((64, 128), bf16)], axis=0)
        own = nn(ROW[j, slab(z), :], square).astype(bf16)
        part = part + nn(own, LT[640 + 128 * j:768 + 128 * j, :])
    DP[...] = part.astype(bf16)

    def piece(owner):
        return (
            pl.ds(pl.multiple_of(lax.rem(owner, strips) * 16, 16), 16),
            pl.ds(pl.multiple_of(lax.div(owner, strips) * wide, 128), wide),
        )

    def send_diag(d):
        rows, columns = piece(col_of(d))
        pltpu.make_async_remote_copy(
            src_ref=DP.at[rows, columns], dst_ref=DRS.at[d - 1],
            send_sem=dsend.at[0], recv_sem=drecv.at[0],
            device_id={"cols": col_of(d)}, device_id_type=MESH,
        ).start()

    def all_in(ref, sem):
        pltpu.make_async_copy(ref, ref, sem).wait()

    each(NC, send_diag)

    weight = []
    for i in range(2):
        for j in range(3):
            block = ACC[j, :, 128 * i:128 * i + 128] * mask[i, j].astype(f32)
            flat = jnp.where(low_lanes(64), pltpu.roll(block[64:, :], 64, 1), 0.0).astype(bf16)
            m = 3 * i + j
            turned = block.T[64:, :]
            if m % 2 == 0:
                turned = jnp.where(low_lanes(64), pltpu.roll(turned, 64, 1), 0.0)
            else:
                turned = jnp.where(low_lanes(64), 0.0, turned)
            weight.append(jnp.concatenate([turned.astype(bf16), jnp.zeros((64, 128), bf16)], axis=0))
            LT[64 * m:64 * m + 64, :] = nt(flat, panel[i, j]).astype(bf16)
    for t in range(3):
        m, n = 2 * t, 2 * t + 1
        MIX[:, 128 * t:128 * t + 128] = (
            nn(panel[m // 3, m % 3], weight[m]) + nn(panel[n // 3, n % 3], weight[n])
        ).astype(bf16)

    def spread(inner):
        keep = low_lanes(192)
        zero = jnp.zeros_like(inner)
        return jnp.concatenate([jnp.where(keep, inner, zero), jnp.where(keep, zero, inner)], axis=0)

    def send_sum(n, terms):
        TS[n] = terms.reshape(half, 2, share, 128)
        copy = pltpu.make_async_remote_copy(
            src_ref=TS.at[n, :, 1 - core], dst_ref=XS.at[n], send_sem=xsend.at[n], recv_sem=xrecv.at[n],
            device_id=other, device_id_type=MESH,
        )
        copy.start()
        return copy

    def pass_sum(n, copy):
        copy.wait_recv()
        YS[n] = TS[n, :, core] + XS[n]

        def send(d):
            pltpu.make_async_remote_copy(
                src_ref=YS.at[n, chip_of(d)], dst_ref=RS.at[n, d - 1],
                send_sem=rsend.at[n], recv_sem=rrecv.at[n],
                device_id={"cols": col_of(2 * d)}, device_id_type=MESH,
            ).start()

        each(half, send)

    def end_sum(n):
        all_in(RS.at[n], rrecv.at[n])
        return YS[n, chip] + jnp.sum(RS[n], axis=0)

    def start_gather(n, whole, own):
        place = whole.at[chip, core]
        place[...] = own

        def send(d):
            pltpu.make_async_remote_copy(
                src_ref=place, dst_ref=place, send_sem=asend.at[n], recv_sem=arecv.at[n],
                device_id={"cols": col_of(2 * d)}, device_id_type=MESH,
            ).start()

        each(half, send)

    def end_gather(n, whole):
        all_in(whole.at[pl.ds(0, half - 1), core], arecv.at[n])
        place = whole.at[:, core]
        copy = pltpu.make_async_remote_copy(
            src_ref=place, dst_ref=place, send_sem=bsend.at[n], recv_sem=brecv.at[n],
            device_id=other, device_id_type=MESH,
        )
        copy.start()
        copy.wait_recv()
        return whole[...].reshape(B, 128)

    def low_share(inner, up):
        total = jnp.zeros((share, 128), f32)
        zero = jnp.zeros((64, 128), bf16)
        for i in range(2):
            half = inner[128 * i + 64:128 * i + 128] if up else inner[128 * i:128 * i + 64]
            keep = low_lanes(64) if i == 0 else jnp.logical_not(low_lanes(64))
            half = jnp.where(keep, half, 0.0).astype(bf16)
            right = jnp.concatenate([half, zero] if up else [zero, half], axis=0)
            total = total + nn(a_low[i, pl.ds(pl.multiple_of(c * share, share), share), :], right)
        return total

    def back_terms(back):
        zero = jnp.zeros((64, 128), bf16)
        total = jnp.zeros((B, 128), f32)
        for j in range(3):
            mine = jnp.where(low_lanes(64), back[64 * j:64 * j + 64], back[192 + 64 * j:256 + 64 * j])
            total = total + nn(ROW[j], jnp.concatenate([mine.astype(bf16), zero], axis=0))
        return total

    nb = B // 128
    strip = lax.rem(c, strips)
    pair = lax.div(strip, 2)
    early = min(2, nb)

    def to_chip(d, group):
        place = FULL.at[group, pair, core, :, columns]
        return pltpu.make_async_remote_copy(
            src_ref=place, dst_ref=place,
            send_sem=csend.at[GROUPS.index(group), d - 1], recv_sem=crecv.at[GROUPS.index(group), d - 1],
            device_id={"cols": col_of(2 * d)}, device_id_type=MESH,
        )

    GROUPS = [pl.ds(0, early)] + ([pl.ds(early, nb - early)] if nb > early else [])

    def to_core(group):
        place = FULL.at[group, :, core]
        return pltpu.make_async_remote_copy(
            src_ref=place, dst_ref=place,
            send_sem=dsend.at[2 + GROUPS.index(group)], recv_sem=drecv.at[2 + GROUPS.index(group)],
            device_id=other, device_id_type=MESH,
        )

    def pass_on(group):
        each(half, lambda d: to_chip(d, group).wait_recv())
        to_core(group).start()

    def block_step(kb):
        o = kb * 128
        rest = o + 128
        top = FULL[kb].reshape(128, B)[:, o:].astype(f32)
        if kb:
            top = top + A[o:rest, o:]
        U, E = yield from chol_block(top[:, :128], 128, 16)
        A[o:rest, o:rest] = U
        Eb = E.astype(bf16)
        INV[kb] = Eb
        if rest < B:
            across = nn(Eb, top[:, 128:].astype(bf16))
            A[o:rest, rest:] = across
            ab = across.astype(bf16)
            LOW[rest:, o:rest] = ab.T
            yield
            for ib in range(kb + 1, nb):
                r = ib * 128
                gone = nn(LOW[r:r + 128, o:rest], ab[:, r - rest:])
                A[r:r + 128, r:] = A[r:r + 128, r:] - gone if kb else -gone
        block = A[o:rest, slab(z)].T
        row = z * 128 + lax.broadcasted_iota(jnp.int32, (128, 128), 0)
        col = o + lax.broadcasted_iota(jnp.int32, (128, 128), 1)
        slab_ref[:, o:rest] = jnp.where(col <= row, block, 0.0)

    to_do = list(range(nb))

    def some_steps(n):
        for _ in range(n):
            if to_do:
                together(block_step(to_do.pop(0)))

    probe = jnp.concatenate([ACC[j, :64, 384:512] for j in range(3)], axis=0)
    x = send_sum(0, nn(MIX[...], spread(probe).astype(bf16)))
    low = low_share(nn(LT[384:640, :], S2[...]), True)
    pass_sum(0, x)
    loads[3].wait()
    all_in(DRS, drecv.at[0])
    rows, columns = piece(c)
    own = a_diag[rows, columns] - (
        DP[rows, columns].astype(f32) + jnp.sum(DRS[...].astype(f32), axis=0)
    )
    FULL[z, pair, core, :, columns] = own.astype(bf16)

    def send_rows(d):
        place = FULL.at[z, pair, core, :, columns]
        pltpu.make_async_remote_copy(
            src_ref=place, dst_ref=place, send_sem=dsend.at[1], recv_sem=drecv.at[1],
            device_id={"rows": row_of(d)}, device_id_type=MESH,
        ).start()

    each(NR, send_rows)
    start_gather(0, FB, (low - end_sum(0)).astype(bf16))
    all_in(FULL.at[pl.ds(0, NR - 1), pair, core, :, columns], drecv.at[1])
    each(half, lambda d: to_chip(d, GROUPS[0]).start())
    first = end_gather(0, FB)

    inner = nn(LT[:640, :], first)
    x = send_sum(1, back_terms(inner[:384]))
    low = low_share(inner[384:], False)
    pass_on(GROUPS[0])
    pass_sum(1, x)
    for group in GROUPS[1:]:
        each(half, lambda d: to_chip(d, group).start())
    to_core(GROUPS[0]).wait_recv()
    some_steps(1)
    start_gather(1, SB, (low - end_sum(1)).astype(bf16))
    some_steps(1)
    second = end_gather(1, SB)

    inner = nn(LT[384:, :], second)
    fore = jnp.concatenate([inner[256 + 128 * j:320 + 128 * j] for j in range(3)], axis=0)
    x = send_sum(2, nn(MIX[...], spread(fore).astype(bf16)))
    low = low_share(inner[:256], True)
    for group in GROUPS[1:]:
        pass_on(group)
    pass_sum(2, x)
    for group in GROUPS[1:]:
        to_core(group).wait_recv()
    some_steps(1)
    start_gather(2, TH, low - end_sum(2))
    some_steps(1)
    third = end_gather(2, TH)

    gram = nn(third.T, third, HIGHEST)
    if to_do:
        inverse, _ = together(inverse_pair(gram), block_step(to_do.pop(0)))
    else:
        inverse, = together(inverse_pair(gram))
    basis = nt(third, inverse, HIGHEST)
    BS[...] = basis

    inner = nn(LT[:640, :], basis.astype(bf16))
    x = send_sum(3, back_terms(inner[:384]))
    low = low_share(inner[384:], False)
    pass_sum(3, x)
    some_steps(1)
    start_gather(3, PB, (low - end_sum(3)).astype(bf16))
    some_steps(nb)
    Y[...] = end_gather(3, PB).astype(f32)

    left = low_lanes(128)
    for kb in range(nb):
        o = kb * 128
        y = nn(INV[kb], Y[o:o + 128, :].astype(bf16))
        if o + 128 < B:
            Y[o + 128:, :] -= nn(LOW[o + 128:, o:o + 128], y.astype(bf16))
        cols = BS[o:o + 128, :]
        panel_ref[0, o:o + 128, :] = jnp.where(left, cols, pltpu.roll(y, 64, 1))
        panel_ref[1, o:o + 128, :] = jnp.where(left, pltpu.roll(cols, 64, 1), y)

    for h in hops:
        h.wait_send()
    all_in(DRS, dsend.at[0])
    all_in(FULL.at[pl.ds(0, NR - 1), pair, core, :, columns], dsend.at[1])
    for group in GROUPS:
        each(half, lambda d: to_chip(d, group).wait_send())
        to_core(group).wait_send()
    for n, whole in enumerate((FB, SB, TH, PB)):
        all_in(XS.at[n], xsend.at[n])
        all_in(RS.at[n], rsend.at[n])
        all_in(whole.at[pl.ds(0, half - 1), core], asend.at[n])
        all_in(whole.at[:, core], bsend.at[n])


def shards(panel, row_k, mask, a_low, a_diag, sketch):
    NC, NR = lax.axis_size("cols"), lax.axis_size("rows")
    B = NR * 128
    share = B // NC
    half = NC // 2
    wide = B // (NC // 8)
    vm = pl.BlockSpec(memory_space=pltpu.VMEM)
    anywhere = pl.BlockSpec(memory_space=pl.ANY)
    dma = pltpu.SemaphoreType.DMA
    shape = jax.ShapeDtypeStruct
    return pl.pallas_call(
        functools.partial(panel_kernel, NC=NC, NR=NR),
        out_shape=(shape((2, B, 128), f32), shape((128, B), f32)),
        in_specs=[anywhere, anywhere, pl.BlockSpec(memory_space=pltpu.SMEM), anywhere, anywhere, vm],
        out_specs=[vm] * 2,
        scratch_shapes=[
            pltpu.VMEM((2, 3, B, 128), bf16),
            pltpu.VMEM((2, B, 128), bf16),
            pltpu.VMEM((128, B), f32),
            pltpu.VMEM((3, B, 128), bf16),
            pltpu.VMEM((1024, B), bf16),
            pltpu.VMEM((3, 128, 512), f32),
            pltpu.VMEM((B, 384), bf16),
            pltpu.VMEM((B, 128), bf16),
            pltpu.VMEM((128, B), bf16),
            pltpu.VMEM((NC - 1, 16, wide), bf16),
            pltpu.VMEM((NR, 4, 2, 16, B), bf16),
            pltpu.VMEM((4, half, 2, share, 128), f32),
            pltpu.VMEM((4, half, share, 128), f32),
            pltpu.VMEM((4, half, share, 128), f32),
            pltpu.VMEM((4, half - 1, share, 128), f32),
            pltpu.VMEM((half, 2, share, 128), bf16),
            pltpu.VMEM((half, 2, share, 128), bf16),
            pltpu.VMEM((half, 2, share, 128), f32),
            pltpu.VMEM((half, 2, share, 128), bf16),
            pltpu.VMEM((B, 128), f32),
            pltpu.VMEM((B, B), f32),
            pltpu.VMEM((B, B), bf16),
            pltpu.VMEM((NR, 128, 128), bf16),
            pltpu.VMEM((B, 128), f32),
            dma((4,)), dma((2, 4, 3)), dma((2, 4, 3)), dma((4,)), dma((4,)),
            dma((2, half)), dma((2, half)),
            dma((4,)), dma((4,)), dma((4,)), dma((4,)), dma((4,)), dma((4,)), dma((4,)), dma((4,)),
        ],
        compiler_params=pltpu.CompilerParams(
            collective_id=0, has_side_effects=True, vmem_limit_bytes=56 * 2**20
        ),
        name="panel",
    )(panel, row_k, mask, a_low, a_diag, sketch)


def solution(mesh):
    return jax.shard_map(
        shards,
        mesh=mesh,
        in_specs=(
            P("rows", "cols", None, None),
            P("cols", "rows", None),
            P("rows", "cols"),
            P("rows", None, None),
            P("rows", None),
            P(),
        ),
        out_specs=(P("rows", None, None), P("rows", None)),
        check_vma=False,
    )
```

```python
import functools

import jax
import jax.numpy as jnp
from jax import lax
from jax.experimental import pallas as pl
from jax.experimental.pallas import tpu as pltpu
from jax.sharding import PartitionSpec as P

f32 = jnp.float32
bf16 = jnp.bfloat16
MESH = pl.DeviceIdType.MESH
HIGHEST = lax.Precision.HIGHEST

def rcp(p):
    r = pl.reciprocal(p, approx=True)
    return r * (2.0 - p * r)

def strip_eliminate(parts, k0, s):
    first = parts[0]
    lanes = first.shape[1]
    row = lax.broadcasted_iota(jnp.int32, (s, lanes), 0)
    C = [jnp.broadcast_to(first[:, k0 + j:k0 + j + 1], (s, lanes)) for j in range(s)]
    parts = list(parts)
    diag = jnp.ones((s, lanes), f32)
    for j in range(s):
        p = C[j][j:j + 1, :]
        diag = jnp.where(row == j, p, diag)
        if j == s - 1: break
        M = jnp.where(row > j, C[j] * rcp(p), 0.0)
        for k in range(j + 1, s):
            C[k] = C[k] - M * C[k][j:j + 1, :]
        parts = [x - M * x[j:j + 1, :] for x in parts]
    R = lax.rsqrt(diag)
    return [x * R for x in parts]

def tn(a, b, prec=None):
    return lax.dot_general(a, b, (((0,), (0,)), ((), ())), preferred_element_type=f32, precision=prec)

def chol_block(D, n, s):
    eye = (lax.broadcasted_iota(jnp.int32, (n, n), 0) == lax.broadcasted_iota(jnp.int32, (n, n), 1)).astype(f32)
    WA, WE = D, eye
    outU, outE = [], []
    for k0 in range(0, n, s):
        a, e = strip_eliminate([WA[:s], WE[:s]], k0, s)
        outU.append(a)
        outE.append(e)
        if k0 + s < n:
            ab = a.astype(bf16)
            eb = e.astype(bf16)
            lhs = ab[:, k0 + s:]
            WA = WA[s:] - tn(lhs, ab)
            WE = WE[s:] - tn(lhs, eb)
            yield
    U = jnp.concatenate(outU, 0)
    E = jnp.concatenate(outE, 0)
    i0 = lax.broadcasted_iota(jnp.int32, (n, n), 0)
    i1 = lax.broadcasted_iota(jnp.int32, (n, n), 1)
    return jnp.where(i1 >= i0, U, 0.0), E


def together(*works):
    given = [None] * len(works)
    live = list(range(len(works)))
    while live:
        for n in list(live):
            try:
                next(works[n])
            except StopIteration as stop:
                given[n] = stop.value
                live.remove(n)
    return given


def inverse_pair(gram):
    n, s = 64, 16
    low = lax.broadcasted_iota(jnp.int32, (s, 128), 1) < n
    row = lax.broadcasted_iota(jnp.int32, (s, 128), 0)
    lanes = lax.broadcasted_iota(jnp.int32, (n, 128), 1)
    left = lanes < n
    A = jnp.where(left, gram[:n], gram[n:])
    E = (lax.rem(lanes, n) == lax.broadcasted_iota(jnp.int32, (n, 128), 0)).astype(f32)
    done = []
    for k0 in range(0, n, s):
        a, e = A[:s], E[:s]
        C = [
            jnp.where(
                low,
                jnp.broadcast_to(a[:, k0 + j:k0 + j + 1], (s, 128)),
                jnp.broadcast_to(a[:, n + k0 + j:n + k0 + j + 1], (s, 128)),
            )
            for j in range(s)
        ]
        diag = jnp.ones((s, 128), f32)
        for j in range(s):
            p = C[j][j:j + 1, :]
            diag = jnp.where(row == j, p, diag)
            if j == s - 1:
                break
            r = rcp(p)
            r = r * (2.0 - p * r)
            M = jnp.where(row > j, C[j] * r, 0.0)
            for k in range(j + 1, s):
                C[k] = C[k] - M * C[k][j:j + 1, :]
            a = a - M * a[j:j + 1, :]
            e = e - M * e[j:j + 1, :]
        R = lax.rsqrt(diag)
        a, e = a * R, e * R
        done.append(e)
        if k0 + s < n:
            both = tn(a, jnp.concatenate([a, e], axis=1), HIGHEST)
            both = [both[:, :128], both[:, 128:]]
            keep = left[k0 + s:]
            step = [jnp.where(keep, x[k0 + s:n], x[n + k0 + s:]) for x in both]
            A, E = A[s:] - step[0], E[s:] - step[1]
            yield
    E = jnp.concatenate(done, axis=0)
    return jnp.concatenate([jnp.where(left, E, 0.0), jnp.where(left, 0.0, E)], axis=0)


def nn(a, b, prec=None):
    return jnp.dot(a, b, preferred_element_type=f32, precision=prec)


def nt(a, b, prec=None):
    return lax.dot_general(a, b, (((1,), (1,)), ((), ())), preferred_element_type=f32, precision=prec)


def low_lanes(n):
    return lax.broadcasted_iota(jnp.int32, (n, 128), 1) < 64


def panel_kernel(
    panel_in, row_in, mask, low_in, diag_in, sketch,
    panel_ref, slab_ref,
    panel, a_low, a_diag, ROW, LT, ACC, MIX, S2, DP, DX, DY, DRS, FULL, TS, XS, YS, RS, FB, SB, TH, PB, BS,
    A, LOW, INV, Y,
    lsem, zsend, zrecv, dsend, drecv, csend, crecv, xsend, xrecv, rsend, rrecv, asend, arecv, bsend, brecv,
    *, NC, NR,
):
    B = NR * 128
    share = B // NC
    half = NC // 2
    strips = 8
    wide = B // (NC // strips)
    c = lax.axis_index("cols")
    z = lax.axis_index("rows")
    core, chip = lax.rem(c, 2), lax.div(c, 2)
    mine = pl.ds(pl.multiple_of(c * share, share), share)
    other = {"cols": c + 1 - 2 * core}
    barrier = pltpu.get_barrier_semaphore()

    def col_of(d):
        return lax.rem(c + d, NC)

    def chip_of(d):
        return lax.rem(chip + d, half)

    def row_of(d):
        return lax.rem(z + d + NR, NR)

    def slab(owner):
        return pl.ds(pl.multiple_of(owner * 128, 128), 128)

    def each(n, body):
        def step(d, carry):
            body(d)
            return carry
        lax.fori_loop(1, n, step, 0)

    loads = [
        pltpu.make_async_copy(row_in, ROW.at[:, slab(z), :], lsem.at[0]),
        pltpu.make_async_copy(panel_in, panel, lsem.at[1]),
        pltpu.make_async_copy(low_in, a_low, lsem.at[2]),
        pltpu.make_async_copy(diag_in, a_diag, lsem.at[3]),
    ]
    for load in loads:
        load.start()
    each(half, lambda d: pl.semaphore_signal(barrier, 1, device_id={"cols": col_of(2 * d)}, device_id_type=MESH))
    pl.semaphore_signal(barrier, 1, device_id=other, device_id_type=MESH)
    each(NR, lambda d: pl.semaphore_signal(barrier, 1, device_id={"rows": row_of(d)}, device_id_type=MESH))
    S2[...] = jnp.concatenate([sketch[...], sketch[...]], axis=0).T
    for j in range(3):
        ACC[j] = jnp.zeros_like(ACC[j])
    loads[0].wait()
    pl.semaphore_wait(barrier, half + NR - 1)

    def hop(way, step, j, owner):
        place = ROW.at[j, slab(owner), :]
        return pltpu.make_async_remote_copy(
            src_ref=place, dst_ref=place,
            send_sem=zsend.at[way, step, j], recv_sem=zrecv.at[way, step, j],
            device_id={"rows": row_of(1 if way == 0 else -1)}, device_id_type=MESH,
        )

    def absorb(owner, j):
        r = ROW[j, slab(owner), :]
        rt = r.T
        LT[640 + 128 * j:768 + 128 * j, slab(owner)] = rt
        right = jnp.concatenate(
            [panel[0, j, slab(owner), :], panel[1, j, slab(owner), :], r, S2[slab(owner), :]], axis=1
        )
        ACC[j] += nn(rt, right)

    last = NR // 2 - 1

    def passes(way, step, j):
        return step < last or (step == last and (way == 0) == (j < 2))

    hops = []
    for j in range(3):
        for way in range(2):
            if passes(way, 0, j):
                hops.append(hop(way, 0, j, z))
                hops[-1].start()
    loads[1].wait()
    for j in range(3):
        absorb(z, j)
    loads[2].wait()
    for i in range(2):
        LT[384 + 128 * i:512 + 128 * i, :] = a_low[i].T
    for s in range(last + 1):
        came = []
        for j in range(3):
            for way in range(2):
                if not passes(way, s, j):
                    continue
                owner = row_of(-1 - s if way == 0 else 1 + s)
                hop(way, s, j, owner).wait_recv()
                if passes(way, s + 1, j):
                    hops.append(hop(way, s + 1, j, owner))
                    hops[-1].start()
                came.append((owner, j))
        for owner, j in came:
            absorb(owner, j)

    part = jnp.zeros((128, B), f32)
    for j in range(3):
        square = pltpu.roll(ACC[j, 64:128, 256:384], 64, 1)
        square = jnp.where(low_lanes(64), square, 0.0).astype(bf16)
        square = jnp.concatenate([square, jnp.zeros((64, 128), bf16)], axis=0)
        own = nn(ROW[j, slab(z), :], square).astype(bf16)
        part = part + nn(own, LT[640 + 128 * j:768 + 128 * j, :])
    DP[...] = part.astype(bf16).reshape(4, 2, 16, B)

    def all_in(ref, sem):
        pltpu.make_async_copy(ref, ref, sem).wait()

    diag_swap = pltpu.make_async_remote_copy(
        src_ref=DP.at[:, 1 - core], dst_ref=DX, send_sem=dsend.at[0], recv_sem=drecv.at[0],
        device_id=other, device_id_type=MESH,
    )
    diag_swap.start()

    def place_of(owner):
        pair = lax.rem(owner, 4)
        return pair, lax.rem(pair + lax.div(owner, 4), NC // strips)

    def columns_of(group):
        return pl.ds(pl.multiple_of(group * wide, 128), wide)

    weight = []
    for i in range(2):
        for j in range(3):
            block = ACC[j, :, 128 * i:128 * i + 128] * mask[i, j].astype(f32)
            flat = jnp.where(low_lanes(64), pltpu.roll(block[64:, :], 64, 1), 0.0).astype(bf16)
            m = 3 * i + j
            turned = block.T[64:, :]
            if m % 2 == 0:
                turned = jnp.where(low_lanes(64), pltpu.roll(turned, 64, 1), 0.0)
            else:
                turned = jnp.where(low_lanes(64), 0.0, turned)
            weight.append(jnp.concatenate([turned.astype(bf16), jnp.zeros((64, 128), bf16)], axis=0))
            LT[64 * m:64 * m + 64, :] = nt(flat, panel[i, j]).astype(bf16)
    for t in range(3):
        m, n = 2 * t, 2 * t + 1
        MIX[:, 128 * t:128 * t + 128] = (
            nn(panel[m // 3, m % 3], weight[m]) + nn(panel[n // 3, n % 3], weight[n])
        ).astype(bf16)

    def spread(inner):
        keep = low_lanes(192)
        zero = jnp.zeros_like(inner)
        return jnp.concatenate([jnp.where(keep, inner, zero), jnp.where(keep, zero, inner)], axis=0)

    def send_sum(n, terms):
        TS[n] = terms.reshape(half, 2, share, 128)
        copy = pltpu.make_async_remote_copy(
            src_ref=TS.at[n, :, 1 - core], dst_ref=XS.at[n], send_sem=xsend.at[n], recv_sem=xrecv.at[n],
            device_id=other, device_id_type=MESH,
        )
        copy.start()
        return copy

    def pass_sum(n, copy):
        copy.wait_recv()
        YS[n] = (TS[n, :, core] + XS[n]).astype(bf16)

        def send(d):
            pltpu.make_async_remote_copy(
                src_ref=YS.at[n, chip_of(d)], dst_ref=RS.at[n, d - 1],
                send_sem=rsend.at[n], recv_sem=rrecv.at[n],
                device_id={"cols": col_of(2 * d)}, device_id_type=MESH,
            ).start()

        each(half, send)

    def end_sum(n):
        all_in(RS.at[n], rrecv.at[n])
        return TS[n, chip, core] + XS[n, chip] + jnp.sum(RS[n].astype(f32), axis=0)

    def start_gather(n, whole, own):
        place = whole.at[chip, core]
        place[...] = own

        def send(d):
            pltpu.make_async_remote_copy(
                src_ref=place, dst_ref=place, send_sem=asend.at[n], recv_sem=arecv.at[n],
                device_id={"cols": col_of(2 * d)}, device_id_type=MESH,
            ).start()

        each(half, send)

    def end_gather(n, whole):
        all_in(whole.at[pl.ds(0, half - 1), core], arecv.at[n])
        place = whole.at[:, core]
        copy = pltpu.make_async_remote_copy(
            src_ref=place, dst_ref=place, send_sem=bsend.at[n], recv_sem=brecv.at[n],
            device_id=other, device_id_type=MESH,
        )
        copy.start()
        copy.wait_recv()
        return whole[...].reshape(B, 128)

    def low_rows(inner, up, rows):
        total = jnp.zeros((rows.size, 128), f32)
        zero = jnp.zeros((64, 128), bf16)
        for i in range(2):
            half = inner[128 * i + 64:128 * i + 128] if up else inner[128 * i:128 * i + 64]
            keep = low_lanes(64) if i == 0 else jnp.logical_not(low_lanes(64))
            half = jnp.where(keep, half, 0.0).astype(bf16)
            right = jnp.concatenate([half, zero] if up else [zero, half], axis=0)
            total = total + nn(a_low[i, rows, :], right)
        return total

    def back_terms(back):
        zero = jnp.zeros((64, 128), bf16)
        total = jnp.zeros((B, 128), f32)
        for j in range(3):
            mine = jnp.where(low_lanes(64), back[64 * j:64 * j + 64], back[192 + 64 * j:256 + 64 * j])
            total = total + nn(ROW[j], jnp.concatenate([mine.astype(bf16), zero], axis=0))
        return total

    nb = B // 128
    pair, group = place_of(chip)
    columns = columns_of(group)

    def to_chip(d, k):
        place = FULL.at[pl.ds(2 * k, 2), pair, core, :, columns]
        return pltpu.make_async_remote_copy(
            src_ref=place, dst_ref=place, send_sem=csend.at[k, d - 1], recv_sem=crecv.at[k, d - 1],
            device_id={"cols": col_of(2 * d)}, device_id_type=MESH,
        )

    def counts(owner, k):
        return (place_of(owner)[1] + 1) * wide > 256 * k

    def spread_group(k):
        @pl.when(counts(chip, k))
        def _():
            each(half, lambda d: to_chip(d, k).start())

    def to_core(k):
        place = FULL.at[pl.ds(2 * k, 2), :, core, :, pl.ds(256 * k, B - 256 * k)]
        return pltpu.make_async_remote_copy(
            src_ref=place, dst_ref=place, send_sem=dsend.at[3 + k], recv_sem=drecv.at[3 + k],
            device_id=other, device_id_type=MESH,
        )

    def pass_on(k):
        def take(d):
            @pl.when(counts(chip_of(half - d), k))
            def _():
                to_chip(d, k).wait_recv()

        each(half, take)
        to_core(k).start()

    def block_step(kb):
        o = kb * 128
        rest = o + 128
        top = FULL[kb].reshape(128, B)[:, o:].astype(f32)
        if kb:
            top = top + A[o:rest, o:]
        U, E = yield from chol_block(top[:, :128], 128, 16)
        A[o:rest, o:rest] = U
        Eb = E.astype(bf16)
        INV[kb] = Eb
        if rest < B:
            across = nn(Eb, top[:, 128:].astype(bf16))
            A[o:rest, rest:] = across
            ab = across.astype(bf16)
            LOW[rest:, o:rest] = ab.T
            yield
            for ib in range(kb + 1, nb):
                r = ib * 128
                gone = nn(LOW[r:r + 128, o:rest], ab[:, r - rest:])
                A[r:r + 128, r:] = A[r:r + 128, r:] - gone if kb else -gone
        block = A[o:rest, slab(z)].T
        row = z * 128 + lax.broadcasted_iota(jnp.int32, (128, 128), 0)
        col = o + lax.broadcasted_iota(jnp.int32, (128, 128), 1)
        slab_ref[:, o:rest] = jnp.where(col <= row, block, 0.0)

    to_do = list(range(nb))

    def some_steps(n):
        for _ in range(n):
            if to_do:
                together(block_step(to_do.pop(0)))

    diag_swap.wait_recv()
    DY[...] = (DP[:, core].astype(f32) + DX[...].astype(f32)).astype(bf16)

    def send_diag(d):
        to_pair, to_group = place_of(chip_of(d))
        pltpu.make_async_remote_copy(
            src_ref=DY.at[to_pair, :, columns_of(to_group)], dst_ref=DRS.at[d - 1],
            send_sem=dsend.at[1], recv_sem=drecv.at[1],
            device_id={"cols": col_of(2 * d)}, device_id_type=MESH,
        ).start()

    probe = jnp.concatenate([ACC[j, :64, 384:512] for j in range(3)], axis=0)
    x = send_sum(0, nn(MIX[...], spread(probe).astype(bf16)))
    low = low_rows(nn(LT[384:640, :], S2[...]), True, mine)
    each(half, send_diag)
    pass_sum(0, x)
    loads[3].wait()
    all_in(DRS, drecv.at[1])
    rows = pl.ds(pl.multiple_of((2 * pair + core) * 16, 16), 16)
    own = a_diag[rows, columns] - (
        DY[pair, :, columns].astype(f32) + jnp.sum(DRS[...].astype(f32), axis=0)
    )
    FULL[z, pair, core, :, columns] = own.astype(bf16)

    def send_rows(d):
        place = FULL.at[z, pair, core, :, columns]
        pltpu.make_async_remote_copy(
            src_ref=place, dst_ref=place, send_sem=dsend.at[2], recv_sem=drecv.at[2],
            device_id={"rows": row_of(d)}, device_id_type=MESH,
        ).start()

    each(NR, send_rows)
    start_gather(0, FB, (low - end_sum(0)).astype(bf16))
    all_in(FULL.at[pl.ds(0, NR - 1), pair, core, :, columns], drecv.at[2])
    spread_group(0)
    first = end_gather(0, FB)

    inner = nn(LT[:640, :], first)
    x = send_sum(1, back_terms(inner[:384]))
    low = low_rows(inner[384:], False, mine)
    pass_on(0)
    pass_sum(1, x)
    for k in range(1, nb // 2):
        spread_group(k)
    to_core(0).wait_recv()
    some_steps(1)
    start_gather(1, SB, (low - end_sum(1)).astype(bf16))
    some_steps(1)
    second = end_gather(1, SB)

    inner = nn(LT[384:, :], second)
    fore = jnp.concatenate([inner[256 + 128 * j:320 + 128 * j] for j in range(3)], axis=0)
    x = send_sum(2, nn(MIX[...], spread(fore).astype(bf16)))
    pass_on(1)
    pass_sum(2, x)
    low = low_rows(inner[:256], True, pl.ds(0, B))
    to_core(1).wait_recv()
    some_steps(1)
    start_gather(2, TH, end_sum(2).astype(bf16))
    for k in range(2, nb // 2):
        pass_on(k)
    some_steps(1)
    third = low - end_gather(2, TH).astype(f32)
    for k in range(2, nb // 2):
        to_core(k).wait_recv()

    gram = nn(third.T, third, HIGHEST)
    if to_do:
        inverse, _ = together(inverse_pair(gram), block_step(to_do.pop(0)))
    else:
        inverse, = together(inverse_pair(gram))
    basis = nt(third, inverse, HIGHEST)
    BS[...] = basis

    inner = nn(LT[:640, :], basis.astype(bf16))
    x = send_sum(3, back_terms(inner[:384]))
    low = low_rows(inner[384:], False, mine)
    pass_sum(3, x)
    some_steps(1)
    start_gather(3, PB, (low - end_sum(3)).astype(bf16))
    some_steps(nb)
    Y[...] = end_gather(3, PB).astype(f32)

    left = low_lanes(128)
    for kb in range(nb):
        o = kb * 128
        y = nn(INV[kb], Y[o:o + 128, :].astype(bf16))
        if o + 128 < B:
            Y[o + 128:, :] -= nn(LOW[o + 128:, o:o + 128], y.astype(bf16))
        cols = BS[o:o + 128, :]
        panel_ref[0, o:o + 128, :] = jnp.where(left, cols, pltpu.roll(y, 64, 1))
        panel_ref[1, o:o + 128, :] = jnp.where(left, pltpu.roll(cols, 64, 1), y)

    for h in hops:
        h.wait_send()
    diag_swap.wait_send()
    all_in(DRS, dsend.at[1])
    all_in(FULL.at[pl.ds(0, NR - 1), pair, core, :, columns], dsend.at[2])
    for k in range(nb // 2):
        @pl.when(counts(chip, k))
        def _():
            each(half, lambda d: to_chip(d, k).wait_send())
        to_core(k).wait_send()
    for n, whole in enumerate((FB, SB, TH, PB)):
        all_in(XS.at[n], xsend.at[n])
        all_in(RS.at[n], rsend.at[n])
        all_in(whole.at[pl.ds(0, half - 1), core], asend.at[n])
        all_in(whole.at[:, core], bsend.at[n])


def out_kernel(panel_in, slab_in, panel_out, slab_out, sems):
    size = slab_in.shape[1] // 4
    copies = []
    for n in range(4):
        cut = pl.ds(size * n, size)
        for i in range(2):
            copies.append((panel_in.at[i, cut], panel_out.at[i, cut]))
        cut = pl.ds(32 * n, 32)
        copies.append((slab_in.at[cut], slab_out.at[cut]))
    copies = [pltpu.make_async_copy(a, b, sems.at[n]) for n, (a, b) in enumerate(copies)]
    for copy in copies:
        copy.start()
    for copy in copies:
        copy.wait()


def written(panel_out, slab):
    anywhere = pl.BlockSpec(memory_space=pl.ANY)
    return pl.pallas_call(
        out_kernel,
        out_shape=(jax.ShapeDtypeStruct(panel_out.shape, f32), jax.ShapeDtypeStruct(slab.shape, f32)),
        in_specs=[anywhere] * 2,
        out_specs=[anywhere] * 2,
        scratch_shapes=[pltpu.SemaphoreType.DMA((12,))],
        compiler_params=pltpu.CompilerParams(vmem_limit_bytes=60 * 2**20),
        name="written",
    )(panel_out, slab)


def shards(panel, row_k, mask, a_low, a_diag, sketch):
    NC, NR = lax.axis_size("cols"), lax.axis_size("rows")
    B = NR * 128
    share = B // NC
    half = NC // 2
    wide = B // (NC // 8)
    vm = pl.BlockSpec(memory_space=pltpu.VMEM)
    anywhere = pl.BlockSpec(memory_space=pl.ANY)
    dma = pltpu.SemaphoreType.DMA
    shape = jax.ShapeDtypeStruct
    outs = pl.pallas_call(
        functools.partial(panel_kernel, NC=NC, NR=NR),
        out_shape=(shape((2, B, 128), f32), shape((128, B), f32)),
        in_specs=[anywhere, anywhere, pl.BlockSpec(memory_space=pltpu.SMEM), anywhere, anywhere, vm],
        out_specs=[vm] * 2,
        scratch_shapes=[
            pltpu.VMEM((2, 3, B, 128), bf16),
            pltpu.VMEM((2, B, 128), bf16),
            pltpu.VMEM((128, B), f32),
            pltpu.VMEM((3, B, 128), bf16),
            pltpu.VMEM((1024, B), bf16),
            pltpu.VMEM((3, 128, 512), f32),
            pltpu.VMEM((B, 384), bf16),
            pltpu.VMEM((B, 128), bf16),
            pltpu.VMEM((4, 2, 16, B), bf16),
            pltpu.VMEM((4, 16, B), bf16),
            pltpu.VMEM((4, 16, B), bf16),
            pltpu.VMEM((half - 1, 16, wide), bf16),
            pltpu.VMEM((NR, 4, 2, 16, B), bf16),
            pltpu.VMEM((4, half, 2, share, 128), f32),
            pltpu.VMEM((4, half, share, 128), f32),
            pltpu.VMEM((4, half, share, 128), bf16),
            pltpu.VMEM((4, half - 1, share, 128), bf16),
            pltpu.VMEM((half, 2, share, 128), bf16),
            pltpu.VMEM((half, 2, share, 128), bf16),
            pltpu.VMEM((half, 2, share, 128), bf16),
            pltpu.VMEM((half, 2, share, 128), bf16),
            pltpu.VMEM((B, 128), f32),
            pltpu.VMEM((B, B), f32),
            pltpu.VMEM((B, B), bf16),
            pltpu.VMEM((NR, 128, 128), bf16),
            pltpu.VMEM((B, 128), f32),
            dma((4,)), dma((2, 4, 3)), dma((2, 4, 3)), dma((3 + NR // 2,)), dma((3 + NR // 2,)),
            dma((NR // 2, half)), dma((NR // 2, half)),
            dma((4,)), dma((4,)), dma((4,)), dma((4,)), dma((4,)), dma((4,)), dma((4,)), dma((4,)),
        ],
        compiler_params=pltpu.CompilerParams(
            collective_id=0, has_side_effects=True, vmem_limit_bytes=56 * 2**20
        ),
        name="panel",
    )(panel, row_k, mask, a_low, a_diag, sketch.T)
    return written(*outs)


def solution(mesh):
    return jax.shard_map(
        shards,
        mesh=mesh,
        in_specs=(
            P("rows", "cols", None, None),
            P("cols", "rows", None),
            P("rows", "cols"),
            P("rows", None, None),
            P("rows", None),
            P(),
        ),
        out_specs=(P("rows", None, None), P("rows", None)),
        check_vma=False,
    )
```

```python
import functools

import jax
import jax.numpy as jnp
from jax import lax
from jax.experimental import pallas as pl
from jax.experimental.pallas import tpu as pltpu
from jax.sharding import PartitionSpec as P

f32 = jnp.float32
bf16 = jnp.bfloat16
MESH = pl.DeviceIdType.MESH
HIGHEST = lax.Precision.HIGHEST

def rcp(p):
    r = pl.reciprocal(p, approx=True)
    return r * (2.0 - p * r)

def strip_eliminate(parts, k0, s):
    first = parts[0]
    lanes = first.shape[1]
    row = lax.broadcasted_iota(jnp.int32, (s, lanes), 0)
    C = [jnp.broadcast_to(first[:, k0 + j:k0 + j + 1], (s, lanes)) for j in range(s)]
    parts = list(parts)
    diag = jnp.ones((s, lanes), f32)

    def spread(x, n):
        return jnp.broadcast_to(x[n:n + 1, :], (8, lanes))

    def tall(x):
        return jnp.concatenate([x] * (s // 8), axis=0)

    p = spread(C[0], 0)
    for j in range(s):
        diag = jnp.where(row == j, tall(p), diag)
        if j == s - 1:
            break
        below = jnp.where(row > j, C[j], 0.0)
        w = spread(C[j], j + 1) * spread(C[j + 1], j)
        q = spread(C[j + 1], j + 1)
        r = pl.reciprocal(p, approx=True)
        u = 2.0 - p * r
        p = q - (w * r) * u
        M = (below * tall(r)) * tall(u)
        for k in range(j + 1, s):
            C[k] = C[k] - M * C[k][j:j + 1, :]
        parts = [x - M * x[j:j + 1, :] for x in parts]
    R = lax.rsqrt(diag)
    return [x * R for x in parts]


def tn(a, b, prec=None):
    return lax.dot_general(a, b, (((0,), (0,)), ((), ())), preferred_element_type=f32, precision=prec)

def chol_block(D, n, s):
    eye = (lax.broadcasted_iota(jnp.int32, (n, n), 0) == lax.broadcasted_iota(jnp.int32, (n, n), 1)).astype(f32)
    WA, WE = D, eye
    outU, outE = [], []
    for k0 in range(0, n, s):
        a, e = strip_eliminate([WA[:s], WE[:s]], k0, s)
        outU.append(a)
        outE.append(e)
        if k0 + s < n:
            ab = a.astype(bf16)
            eb = e.astype(bf16)
            lhs = ab[:, k0 + s:]
            WA = WA[s:] - tn(lhs, ab)
            WE = WE[s:] - tn(lhs, eb)
            yield
    U = jnp.concatenate(outU, 0)
    E = jnp.concatenate(outE, 0)
    i0 = lax.broadcasted_iota(jnp.int32, (n, n), 0)
    i1 = lax.broadcasted_iota(jnp.int32, (n, n), 1)
    return jnp.where(i1 >= i0, U, 0.0), E


def together(*works):
    given = [None] * len(works)
    live = list(range(len(works)))
    while live:
        for n in list(live):
            try:
                next(works[n])
            except StopIteration as stop:
                given[n] = stop.value
                live.remove(n)
    return given


def inverse_pair(gram):
    n, s = 64, 16
    low = lax.broadcasted_iota(jnp.int32, (s, 128), 1) < n
    row = lax.broadcasted_iota(jnp.int32, (s, 128), 0)
    lanes = lax.broadcasted_iota(jnp.int32, (n, 128), 1)
    left = lanes < n
    A = jnp.where(left, gram[:n], gram[n:])
    E = (lax.rem(lanes, n) == lax.broadcasted_iota(jnp.int32, (n, 128), 0)).astype(f32)
    done = []
    for k0 in range(0, n, s):
        a, e = A[:s], E[:s]
        C = [
            jnp.where(
                low,
                jnp.broadcast_to(a[:, k0 + j:k0 + j + 1], (s, 128)),
                jnp.broadcast_to(a[:, n + k0 + j:n + k0 + j + 1], (s, 128)),
            )
            for j in range(s)
        ]
        diag = jnp.ones((s, 128), f32)
        for j in range(s):
            p = C[j][j:j + 1, :]
            diag = jnp.where(row == j, p, diag)
            if j == s - 1:
                break
            r = rcp(p)
            r = r * (2.0 - p * r)
            M = jnp.where(row > j, C[j] * r, 0.0)
            for k in range(j + 1, s):
                C[k] = C[k] - M * C[k][j:j + 1, :]
            a = a - M * a[j:j + 1, :]
            e = e - M * e[j:j + 1, :]
        R = lax.rsqrt(diag)
        a, e = a * R, e * R
        done.append(e)
        if k0 + s < n:
            both = tn(a, jnp.concatenate([a, e], axis=1), HIGHEST)
            both = [both[:, :128], both[:, 128:]]
            keep = left[k0 + s:]
            step = [jnp.where(keep, x[k0 + s:n], x[n + k0 + s:]) for x in both]
            A, E = A[s:] - step[0], E[s:] - step[1]
            yield
    E = jnp.concatenate(done, axis=0)
    return jnp.concatenate([jnp.where(left, E, 0.0), jnp.where(left, 0.0, E)], axis=0)


def nn(a, b, prec=None):
    return jnp.dot(a, b, preferred_element_type=f32, precision=prec)


def nt(a, b, prec=None):
    return lax.dot_general(a, b, (((1,), (1,)), ((), ())), preferred_element_type=f32, precision=prec)


def low_lanes(n):
    return lax.broadcasted_iota(jnp.int32, (n, 128), 1) < 64


def panel_kernel(
    panel_in, row_in, mask, low_in, diag_in, sketch,
    panel_ref, slab_ref,
    panel, a_low, a_diag, ROW, LT, ACC, MIX, S2, DP, DX, DY, DRS, FULL, TS, XS, YS, RS, FB, SB, TH, PB, BS,
    A, LOW, INV, Y,
    lsem, zsend, zrecv, dsend, drecv, csend, crecv, xsend, xrecv, rsend, rrecv, asend, arecv, bsend, brecv,
    *, NC, NR,
):
    B = NR * 128
    share = B // NC
    half = NC // 2
    strips = 8
    wide = B // (NC // strips)
    c = lax.axis_index("cols")
    z = lax.axis_index("rows")
    core, chip = lax.rem(c, 2), lax.div(c, 2)
    mine = pl.ds(pl.multiple_of(c * share, share), share)
    other = {"cols": c + 1 - 2 * core}
    barrier = pltpu.get_barrier_semaphore()

    def col_of(d):
        return lax.rem(c + d, NC)

    def chip_of(d):
        return lax.rem(chip + d, half)

    def row_of(d):
        return lax.rem(z + d + NR, NR)

    def slab(owner):
        return pl.ds(pl.multiple_of(owner * 128, 128), 128)

    def each(n, body):
        def step(d, carry):
            body(d)
            return carry
        lax.fori_loop(1, n, step, 0)

    loads = [
        pltpu.make_async_copy(row_in, ROW.at[:, slab(z), :], lsem.at[0]),
        pltpu.make_async_copy(panel_in, panel, lsem.at[1]),
        pltpu.make_async_copy(low_in, a_low, lsem.at[2]),
        pltpu.make_async_copy(diag_in, a_diag, lsem.at[3]),
    ]
    for load in loads:
        load.start()
    each(half, lambda d: pl.semaphore_signal(barrier, 1, device_id={"cols": col_of(2 * d)}, device_id_type=MESH))
    pl.semaphore_signal(barrier, 1, device_id=other, device_id_type=MESH)
    each(NR, lambda d: pl.semaphore_signal(barrier, 1, device_id={"rows": row_of(d)}, device_id_type=MESH))
    S2[...] = jnp.concatenate([sketch[...], sketch[...]], axis=0).T
    for j in range(3):
        ACC[j] = jnp.zeros_like(ACC[j])
    loads[0].wait()
    pl.semaphore_wait(barrier, half + NR - 1)

    def hop(way, step, j, owner):
        place = ROW.at[j, slab(owner), :]
        return pltpu.make_async_remote_copy(
            src_ref=place, dst_ref=place,
            send_sem=zsend.at[way, step, j], recv_sem=zrecv.at[way, step, j],
            device_id={"rows": row_of(1 if way == 0 else -1)}, device_id_type=MESH,
        )

    def absorb(owner, j):
        r = ROW[j, slab(owner), :]
        rt = r.T
        LT[640 + 128 * j:768 + 128 * j, slab(owner)] = rt
        right = jnp.concatenate(
            [panel[0, j, slab(owner), :], panel[1, j, slab(owner), :], r, S2[slab(owner), :]], axis=1
        )
        ACC[j] += nn(rt, right)

    last = NR // 2 - 1

    def passes(way, step, j):
        return step < last or (step == last and (way == 0) == (j < 2))

    hops = []
    for j in range(3):
        for way in range(2):
            if passes(way, 0, j):
                hops.append(hop(way, 0, j, z))
                hops[-1].start()
    loads[1].wait()
    for j in range(3):
        absorb(z, j)
    loads[2].wait()
    for i in range(2):
        LT[384 + 128 * i:512 + 128 * i, :] = a_low[i].T
    came = []
    for s in range(last + 1):
        for j in range(3):
            for way in range(2):
                if not passes(way, s, j):
                    continue
                owner = row_of(-1 - s if way == 0 else 1 + s)
                hop(way, s, j, owner).wait_recv()
                if passes(way, s + 1, j):
                    hops.append(hop(way, s + 1, j, owner))
                    hops[-1].start()
                if came:
                    absorb(*came.pop())
                came.append((owner, j))
    absorb(*came.pop())

    part = jnp.zeros((128, B), f32)
    for j in range(3):
        square = pltpu.roll(ACC[j, 64:128, 256:384], 64, 1)
        square = jnp.where(low_lanes(64), square, 0.0).astype(bf16)
        square = jnp.concatenate([square, jnp.zeros((64, 128), bf16)], axis=0)
        own = nn(ROW[j, slab(z), :], square).astype(bf16)
        part = part + nn(own, LT[640 + 128 * j:768 + 128 * j, :])
    DP[...] = part.astype(bf16).reshape(4, 2, 16, B)

    def all_in(ref, sem):
        pltpu.make_async_copy(ref, ref, sem).wait()

    diag_swap = pltpu.make_async_remote_copy(
        src_ref=DP.at[:, 1 - core], dst_ref=DX, send_sem=dsend.at[0], recv_sem=drecv.at[0],
        device_id=other, device_id_type=MESH,
    )
    diag_swap.start()

    def place_of(owner):
        pair = lax.rem(owner, 4)
        return pair, lax.rem(pair + lax.div(owner, 4), NC // strips)

    def columns_of(group):
        return pl.ds(pl.multiple_of(group * wide, 128), wide)

    weight = []
    for i in range(2):
        for j in range(3):
            block = ACC[j, :, 128 * i:128 * i + 128] * mask[i, j].astype(f32)
            flat = jnp.where(low_lanes(64), pltpu.roll(block[64:, :], 64, 1), 0.0).astype(bf16)
            m = 3 * i + j
            turned = block.T[64:, :]
            if m % 2 == 0:
                turned = jnp.where(low_lanes(64), pltpu.roll(turned, 64, 1), 0.0)
            else:
                turned = jnp.where(low_lanes(64), 0.0, turned)
            weight.append(jnp.concatenate([turned.astype(bf16), jnp.zeros((64, 128), bf16)], axis=0))
            LT[64 * m:64 * m + 64, :] = nt(flat, panel[i, j]).astype(bf16)
    for t in range(3):
        m, n = 2 * t, 2 * t + 1
        MIX[:, 128 * t:128 * t + 128] = (
            nn(panel[m // 3, m % 3], weight[m]) + nn(panel[n // 3, n % 3], weight[n])
        ).astype(bf16)

    def spread(inner):
        keep = low_lanes(192)
        zero = jnp.zeros_like(inner)
        return jnp.concatenate([jnp.where(keep, inner, zero), jnp.where(keep, zero, inner)], axis=0)

    def send_sum(n, terms):
        TS[n] = terms.reshape(half, 2, share, 128)
        copy = pltpu.make_async_remote_copy(
            src_ref=TS.at[n, :, 1 - core], dst_ref=XS.at[n], send_sem=xsend.at[n], recv_sem=xrecv.at[n],
            device_id=other, device_id_type=MESH,
        )
        copy.start()
        return copy

    def pass_sum(n, copy):
        copy.wait_recv()
        YS[n] = (TS[n, :, core] + XS[n]).astype(bf16)

        def send(d):
            pltpu.make_async_remote_copy(
                src_ref=YS.at[n, chip_of(d)], dst_ref=RS.at[n, d - 1],
                send_sem=rsend.at[n], recv_sem=rrecv.at[n],
                device_id={"cols": col_of(2 * d)}, device_id_type=MESH,
            ).start()

        each(half, send)

    def end_sum(n):
        all_in(RS.at[n], rrecv.at[n])
        return TS[n, chip, core] + XS[n, chip] + jnp.sum(RS[n].astype(f32), axis=0)

    def start_gather(n, whole, own):
        place = whole.at[chip, core]
        place[...] = own

        def send(d):
            pltpu.make_async_remote_copy(
                src_ref=place, dst_ref=place, send_sem=asend.at[n], recv_sem=arecv.at[n],
                device_id={"cols": col_of(2 * d)}, device_id_type=MESH,
            ).start()

        each(half, send)

    def end_gather(n, whole):
        all_in(whole.at[pl.ds(0, half - 1), core], arecv.at[n])
        place = whole.at[:, core]
        copy = pltpu.make_async_remote_copy(
            src_ref=place, dst_ref=place, send_sem=bsend.at[n], recv_sem=brecv.at[n],
            device_id=other, device_id_type=MESH,
        )
        copy.start()
        copy.wait_recv()
        return whole[...].reshape(B, 128)

    def low_rows(inner, up, rows):
        total = jnp.zeros((rows.size, 128), f32)
        zero = jnp.zeros((64, 128), bf16)
        for i in range(2):
            half = inner[128 * i + 64:128 * i + 128] if up else inner[128 * i:128 * i + 64]
            keep = low_lanes(64) if i == 0 else jnp.logical_not(low_lanes(64))
            half = jnp.where(keep, half, 0.0).astype(bf16)
            right = jnp.concatenate([half, zero] if up else [zero, half], axis=0)
            total = total + nn(a_low[i, rows, :], right)
        return total

    def back_terms(back):
        zero = jnp.zeros((64, 128), bf16)
        total = jnp.zeros((B, 128), f32)
        for j in range(3):
            mine = jnp.where(low_lanes(64), back[64 * j:64 * j + 64], back[192 + 64 * j:256 + 64 * j])
            total = total + nn(ROW[j], jnp.concatenate([mine.astype(bf16), zero], axis=0))
        return total

    nb = B // 128
    pair, group = place_of(chip)
    columns = columns_of(group)

    def to_chip(d, k):
        place = FULL.at[pl.ds(2 * k, 2), pair, core, :, columns]
        return pltpu.make_async_remote_copy(
            src_ref=place, dst_ref=place, send_sem=csend.at[k, d - 1], recv_sem=crecv.at[k, d - 1],
            device_id={"cols": col_of(2 * d)}, device_id_type=MESH,
        )

    def counts(owner, k):
        return (place_of(owner)[1] + 1) * wide > 256 * k

    def spread_group(k):
        @pl.when(counts(chip, k))
        def _():
            each(half, lambda d: to_chip(d, k).start())

    def to_core(k):
        place = FULL.at[pl.ds(2 * k, 2), :, core, :, pl.ds(256 * k, B - 256 * k)]
        return pltpu.make_async_remote_copy(
            src_ref=place, dst_ref=place, send_sem=dsend.at[3 + k], recv_sem=drecv.at[3 + k],
            device_id=other, device_id_type=MESH,
        )

    def pass_on(k):
        def take(d):
            @pl.when(counts(chip_of(half - d), k))
            def _():
                to_chip(d, k).wait_recv()

        each(half, take)
        to_core(k).start()

    def block_step(kb):
        o = kb * 128
        rest = o + 128
        top = FULL[kb].reshape(128, B)[:, o:].astype(f32)
        if kb:
            top = top + A[o:rest, o:]
        U, E = yield from chol_block(top[:, :128], 128, 16)
        A[o:rest, o:rest] = U
        Eb = E.astype(bf16)
        INV[kb] = Eb
        if rest < B:
            across = nn(Eb, top[:, 128:].astype(bf16))
            A[o:rest, rest:] = across
            ab = across.astype(bf16)
            LOW[rest:, o:rest] = ab.T
            yield
            for ib in range(kb + 1, nb):
                r = ib * 128
                gone = nn(LOW[r:r + 128, o:rest], ab[:, r - rest:])
                A[r:r + 128, r:] = A[r:r + 128, r:] - gone if kb else -gone
        block = A[o:rest, slab(z)].T
        row = z * 128 + lax.broadcasted_iota(jnp.int32, (128, 128), 0)
        col = o + lax.broadcasted_iota(jnp.int32, (128, 128), 1)
        slab_ref[:, o:rest] = jnp.where(col <= row, block, 0.0)

    to_do = list(range(nb))

    def some_steps(n):
        for _ in range(n):
            if to_do:
                together(block_step(to_do.pop(0)))

    diag_swap.wait_recv()
    DY[...] = (DP[:, core].astype(f32) + DX[...].astype(f32)).astype(bf16)

    def send_diag(d):
        to_pair, to_group = place_of(chip_of(d))
        pltpu.make_async_remote_copy(
            src_ref=DY.at[to_pair, :, columns_of(to_group)], dst_ref=DRS.at[d - 1],
            send_sem=dsend.at[1], recv_sem=drecv.at[1],
            device_id={"cols": col_of(2 * d)}, device_id_type=MESH,
        ).start()

    probe = jnp.concatenate([ACC[j, :64, 384:512] for j in range(3)], axis=0)
    x = send_sum(0, nn(MIX[...], spread(probe).astype(bf16)))
    low = low_rows(nn(LT[384:640, :], S2[...]), True, mine)
    each(half, send_diag)
    pass_sum(0, x)
    loads[3].wait()
    all_in(DRS, drecv.at[1])
    rows = pl.ds(pl.multiple_of((2 * pair + core) * 16, 16), 16)
    own = a_diag[rows, columns] - (
        DY[pair, :, columns].astype(f32) + jnp.sum(DRS[...].astype(f32), axis=0)
    )
    FULL[z, pair, core, :, columns] = own.astype(bf16)

    def send_rows(d):
        place = FULL.at[z, pair, core, :, columns]
        pltpu.make_async_remote_copy(
            src_ref=place, dst_ref=place, send_sem=dsend.at[2], recv_sem=drecv.at[2],
            device_id={"rows": row_of(d)}, device_id_type=MESH,
        ).start()

    each(NR, send_rows)
    start_gather(0, FB, (low - end_sum(0)).astype(bf16))
    all_in(FULL.at[pl.ds(0, NR - 1), pair, core, :, columns], drecv.at[2])
    spread_group(0)
    first = end_gather(0, FB)

    inner = nn(LT[:640, :], first)
    x = send_sum(1, back_terms(inner[:384]))
    low = low_rows(inner[384:], False, mine)
    pass_on(0)
    pass_sum(1, x)
    for k in range(1, nb // 2):
        spread_group(k)
    to_core(0).wait_recv()
    some_steps(1)
    start_gather(1, SB, (low - end_sum(1)).astype(bf16))
    some_steps(1)
    second = end_gather(1, SB)

    inner = nn(LT[384:, :], second)
    fore = jnp.concatenate([inner[256 + 128 * j:320 + 128 * j] for j in range(3)], axis=0)
    x = send_sum(2, nn(MIX[...], spread(fore).astype(bf16)))
    pass_on(1)
    pass_sum(2, x)
    low = low_rows(inner[:256], True, pl.ds(0, B))
    to_core(1).wait_recv()
    some_steps(1)
    start_gather(2, TH, end_sum(2).astype(bf16))
    for k in range(2, nb // 2):
        pass_on(k)
    some_steps(1)
    third = low - end_gather(2, TH).astype(f32)
    for k in range(2, nb // 2):
        to_core(k).wait_recv()

    gram = nn(third.T, third, HIGHEST)
    if to_do:
        inverse, _ = together(inverse_pair(gram), block_step(to_do.pop(0)))
    else:
        inverse, = together(inverse_pair(gram))
    basis = nt(third, inverse, HIGHEST)
    BS[...] = basis

    inner = nn(LT[:640, :], basis.astype(bf16))
    x = send_sum(3, back_terms(inner[:384]))
    low = low_rows(inner[384:], False, mine)
    pass_sum(3, x)
    some_steps(1)
    start_gather(3, PB, (low - end_sum(3)).astype(bf16))
    some_steps(nb)
    Y[...] = end_gather(3, PB).astype(f32)

    left = low_lanes(128)
    for kb in range(nb):
        o = kb * 128
        y = nn(INV[kb], Y[o:o + 128, :].astype(bf16))
        if o + 128 < B:
            Y[o + 128:, :] -= nn(LOW[o + 128:, o:o + 128], y.astype(bf16))
        cols = BS[o:o + 128, :]
        panel_ref[0, o:o + 128, :] = jnp.where(left, cols, pltpu.roll(y, 64, 1))
        panel_ref[1, o:o + 128, :] = jnp.where(left, pltpu.roll(cols, 64, 1), y)

    for h in hops:
        h.wait_send()
    diag_swap.wait_send()
    all_in(DRS, dsend.at[1])
    all_in(FULL.at[pl.ds(0, NR - 1), pair, core, :, columns], dsend.at[2])
    for k in range(nb // 2):
        @pl.when(counts(chip, k))
        def _():
            each(half, lambda d: to_chip(d, k).wait_send())
        to_core(k).wait_send()
    for n, whole in enumerate((FB, SB, TH, PB)):
        all_in(XS.at[n], xsend.at[n])
        all_in(RS.at[n], rsend.at[n])
        all_in(whole.at[pl.ds(0, half - 1), core], asend.at[n])
        all_in(whole.at[:, core], bsend.at[n])


def out_kernel(panel_in, slab_in, panel_out, slab_out):
    panel_out[...] = panel_in[...]
    slab_out[...] = slab_in[...]


def written(panel_out, slab):
    n = panel_out.shape[1] // 4
    blocks = [pl.BlockSpec((2, n, 128), lambda i: (0, i, 0)), pl.BlockSpec((32, slab.shape[1]), lambda i: (i, 0))]
    return pl.pallas_call(
        out_kernel,
        grid=(4,),
        out_shape=(jax.ShapeDtypeStruct(panel_out.shape, f32), jax.ShapeDtypeStruct(slab.shape, f32)),
        in_specs=blocks,
        out_specs=blocks,
        name="written",
    )(panel_out, slab)


def shards(panel, row_k, mask, a_low, a_diag, sketch):
    NC, NR = lax.axis_size("cols"), lax.axis_size("rows")
    B = NR * 128
    share = B // NC
    half = NC // 2
    wide = B // (NC // 8)
    vm = pl.BlockSpec(memory_space=pltpu.VMEM)
    anywhere = pl.BlockSpec(memory_space=pl.ANY)
    dma = pltpu.SemaphoreType.DMA
    shape = jax.ShapeDtypeStruct
    outs = pl.pallas_call(
        functools.partial(panel_kernel, NC=NC, NR=NR),
        out_shape=(shape((2, B, 128), f32), shape((128, B), f32)),
        in_specs=[anywhere, anywhere, pl.BlockSpec(memory_space=pltpu.SMEM), anywhere, anywhere, vm],
        out_specs=[vm] * 2,
        scratch_shapes=[
            pltpu.VMEM((2, 3, B, 128), bf16),
            pltpu.VMEM((2, B, 128), bf16),
            pltpu.VMEM((128, B), f32),
            pltpu.VMEM((3, B, 128), bf16),
            pltpu.VMEM((1024, B), bf16),
            pltpu.VMEM((3, 128, 512), f32),
            pltpu.VMEM((B, 384), bf16),
            pltpu.VMEM((B, 128), bf16),
            pltpu.VMEM((4, 2, 16, B), bf16),
            pltpu.VMEM((4, 16, B), bf16),
            pltpu.VMEM((4, 16, B), bf16),
            pltpu.VMEM((half - 1, 16, wide), bf16),
            pltpu.VMEM((NR, 4, 2, 16, B), bf16),
            pltpu.VMEM((4, half, 2, share, 128), f32),
            pltpu.VMEM((4, half, share, 128), f32),
            pltpu.VMEM((4, half, share, 128), bf16),
            pltpu.VMEM((4, half - 1, share, 128), bf16),
            pltpu.VMEM((half, 2, share, 128), bf16),
            pltpu.VMEM((half, 2, share, 128), bf16),
            pltpu.VMEM((half, 2, share, 128), bf16),
            pltpu.VMEM((half, 2, share, 128), bf16),
            pltpu.VMEM((B, 128), f32),
            pltpu.VMEM((B, B), f32),
            pltpu.VMEM((B, B), bf16),
            pltpu.VMEM((NR, 128, 128), bf16),
            pltpu.VMEM((B, 128), f32),
            dma((4,)), dma((2, 4, 3)), dma((2, 4, 3)), dma((3 + NR // 2,)), dma((3 + NR // 2,)),
            dma((NR // 2, half)), dma((NR // 2, half)),
            dma((4,)), dma((4,)), dma((4,)), dma((4,)), dma((4,)), dma((4,)), dma((4,)), dma((4,)),
        ],
        compiler_params=pltpu.CompilerParams(
            collective_id=0, has_side_effects=True, vmem_limit_bytes=56 * 2**20
        ),
        name="panel",
    )(panel, row_k, mask, a_low, a_diag, sketch.T)
    return written(*outs)


def solution(mesh):
    return jax.shard_map(
        shards,
        mesh=mesh,
        in_specs=(
            P("rows", "cols", None, None),
            P("cols", "rows", None),
            P("rows", "cols"),
            P("rows", None, None),
            P("rows", None),
            P(),
        ),
        out_specs=(P("rows", None, None), P("rows", None)),
        check_vma=False,
    )
```

```python
import functools

import jax
import jax.numpy as jnp
from jax import lax
from jax.experimental import pallas as pl
from jax.experimental.pallas import tpu as pltpu
from jax.sharding import PartitionSpec as P

f32 = jnp.float32
bf16 = jnp.bfloat16
MESH = pl.DeviceIdType.MESH
HIGHEST = lax.Precision.HIGHEST

def rcp(p):
    r = pl.reciprocal(p, approx=True)
    return r * (2.0 - p * r)

def strip_eliminate(parts, k0, s):
    first = parts[0]
    lanes = first.shape[1]
    row = lax.broadcasted_iota(jnp.int32, (s, lanes), 0)
    C = [jnp.broadcast_to(first[:, k0 + j:k0 + j + 1], (s, lanes)) for j in range(s)]
    parts = list(parts)
    diag = jnp.ones((s, lanes), f32)

    def spread(x, n):
        return jnp.broadcast_to(x[n:n + 1, :], (8, lanes))

    def tall(x):
        return jnp.concatenate([x] * (s // 8), axis=0)

    p = spread(C[0], 0)
    for j in range(s):
        diag = jnp.where(row == j, tall(p), diag)
        if j == s - 1:
            break
        below = jnp.where(row > j, C[j], 0.0)
        w = spread(C[j], j + 1) * spread(C[j + 1], j)
        q = spread(C[j + 1], j + 1)
        r = pl.reciprocal(p, approx=True)
        u = 2.0 - p * r
        p = q - (w * r) * u
        M = (below * tall(r)) * tall(u)
        for k in range(j + 1, s):
            C[k] = C[k] - M * C[k][j:j + 1, :]
        parts = [x - M * x[j:j + 1, :] for x in parts]
    R = lax.rsqrt(diag)
    return [x * R for x in parts]


def tn(a, b, prec=None):
    return lax.dot_general(a, b, (((0,), (0,)), ((), ())), preferred_element_type=f32, precision=prec)

def chol_block(D, n, s):
    eye = (lax.broadcasted_iota(jnp.int32, (n, n), 0) == lax.broadcasted_iota(jnp.int32, (n, n), 1)).astype(f32)
    WA, WE = D, eye
    outU, outE = [], []
    for k0 in range(0, n, s):
        a, e = strip_eliminate([WA[:s], WE[:s]], k0, s)
        outU.append(a)
        outE.append(e)
        if k0 + s < n:
            ab = a.astype(bf16)
            eb = e.astype(bf16)
            lhs = ab[:, k0 + s:]
            WA = WA[s:] - tn(lhs, ab)
            WE = WE[s:] - tn(lhs, eb)
            yield
    U = jnp.concatenate(outU, 0)
    E = jnp.concatenate(outE, 0)
    i0 = lax.broadcasted_iota(jnp.int32, (n, n), 0)
    i1 = lax.broadcasted_iota(jnp.int32, (n, n), 1)
    return jnp.where(i1 >= i0, U, 0.0), E


def together(*works):
    given = [None] * len(works)
    live = list(range(len(works)))
    while live:
        for n in list(live):
            try:
                next(works[n])
            except StopIteration as stop:
                given[n] = stop.value
                live.remove(n)
    return given


def inverse_pair(gram):
    n, s = 64, 16
    low = lax.broadcasted_iota(jnp.int32, (s, 128), 1) < n
    row = lax.broadcasted_iota(jnp.int32, (s, 128), 0)
    lanes = lax.broadcasted_iota(jnp.int32, (n, 128), 1)
    left = lanes < n
    A = jnp.where(left, gram[:n], gram[n:])
    E = (lax.rem(lanes, n) == lax.broadcasted_iota(jnp.int32, (n, 128), 0)).astype(f32)
    done = []
    for k0 in range(0, n, s):
        a, e = A[:s], E[:s]
        C = [
            jnp.where(
                low,
                jnp.broadcast_to(a[:, k0 + j:k0 + j + 1], (s, 128)),
                jnp.broadcast_to(a[:, n + k0 + j:n + k0 + j + 1], (s, 128)),
            )
            for j in range(s)
        ]
        diag = jnp.ones((s, 128), f32)
        for j in range(s):
            p = C[j][j:j + 1, :]
            diag = jnp.where(row == j, p, diag)
            if j == s - 1:
                break
            r = rcp(p)
            r = r * (2.0 - p * r)
            M = jnp.where(row > j, C[j] * r, 0.0)
            for k in range(j + 1, s):
                C[k] = C[k] - M * C[k][j:j + 1, :]
            a = a - M * a[j:j + 1, :]
            e = e - M * e[j:j + 1, :]
        R = lax.rsqrt(diag)
        a, e = a * R, e * R
        done.append(e)
        if k0 + s < n:
            both = tn(a, jnp.concatenate([a, e], axis=1), HIGHEST)
            both = [both[:, :128], both[:, 128:]]
            keep = left[k0 + s:]
            step = [jnp.where(keep, x[k0 + s:n], x[n + k0 + s:]) for x in both]
            A, E = A[s:] - step[0], E[s:] - step[1]
            yield
    E = jnp.concatenate(done, axis=0)
    return jnp.concatenate([jnp.where(left, E, 0.0), jnp.where(left, 0.0, E)], axis=0)


def nn(a, b, prec=None):
    return jnp.dot(a, b, preferred_element_type=f32, precision=prec)


def nt(a, b, prec=None):
    return lax.dot_general(a, b, (((1,), (1,)), ((), ())), preferred_element_type=f32, precision=prec)


def low_lanes(n):
    return lax.broadcasted_iota(jnp.int32, (n, 128), 1) < 64


def panel_kernel(
    panel_in, row_in, mask, low_in, diag_in, sketch,
    panel_out, slab_out,
    panel_ref, slab_ref, panel, a_low, a_diag, ROW, LT, ACC, MIX, S2, DP, DX, DY, DRS, FULL, TS, XS, YS, RS, FB, SB, TH, PB, BS,
    A, LOW, INV, Y,
    lsem, osem, zsend, zrecv, dsend, drecv, csend, crecv, xsend, xrecv, rsend, rrecv, asend, arecv, bsend, brecv,
    *, NC, NR,
):
    B = NR * 128
    share = B // NC
    half = NC // 2
    strips = 8
    wide = B // (NC // strips)
    c = lax.axis_index("cols")
    z = lax.axis_index("rows")
    core, chip = lax.rem(c, 2), lax.div(c, 2)
    mine = pl.ds(pl.multiple_of(c * share, share), share)
    other = {"cols": c + 1 - 2 * core}
    barrier = pltpu.get_barrier_semaphore()

    def col_of(d):
        return lax.rem(c + d, NC)

    def chip_of(d):
        return lax.rem(chip + d, half)

    def row_of(d):
        return lax.rem(z + d + NR, NR)

    def slab(owner):
        return pl.ds(pl.multiple_of(owner * 128, 128), 128)

    def each(n, body):
        def step(d, carry):
            body(d)
            return carry
        lax.fori_loop(1, n, step, 0)

    loads = [
        pltpu.make_async_copy(row_in, ROW.at[:, slab(z), :], lsem.at[0]),
        pltpu.make_async_copy(panel_in, panel, lsem.at[1]),
        pltpu.make_async_copy(low_in, a_low, lsem.at[2]),
        pltpu.make_async_copy(diag_in, a_diag, lsem.at[3]),
    ]
    for load in loads:
        load.start()
    each(half, lambda d: pl.semaphore_signal(barrier, 1, device_id={"cols": col_of(2 * d)}, device_id_type=MESH))
    pl.semaphore_signal(barrier, 1, device_id=other, device_id_type=MESH)
    each(NR, lambda d: pl.semaphore_signal(barrier, 1, device_id={"rows": row_of(d)}, device_id_type=MESH))
    S2[...] = jnp.concatenate([sketch[...], sketch[...]], axis=0).T
    for j in range(3):
        ACC[j] = jnp.zeros_like(ACC[j])
    loads[0].wait()
    pl.semaphore_wait(barrier, half + NR - 1)

    def hop(way, step, j, owner):
        place = ROW.at[j, slab(owner), :]
        return pltpu.make_async_remote_copy(
            src_ref=place, dst_ref=place,
            send_sem=zsend.at[way, step, j], recv_sem=zrecv.at[way, step, j],
            device_id={"rows": row_of(1 if way == 0 else -1)}, device_id_type=MESH,
        )

    def absorb(owner, j):
        r = ROW[j, slab(owner), :]
        rt = r.T
        LT[640 + 128 * j:768 + 128 * j, slab(owner)] = rt
        right = jnp.concatenate(
            [panel[0, j, slab(owner), :], panel[1, j, slab(owner), :], r, S2[slab(owner), :]], axis=1
        )
        ACC[j] += nn(rt, right)

    last = NR // 2 - 1

    def passes(way, step, j):
        return step < last or (step == last and (way == 0) == (j < 2))

    hops = []
    for j in range(3):
        for way in range(2):
            if passes(way, 0, j):
                hops.append(hop(way, 0, j, z))
                hops[-1].start()
    loads[1].wait()
    for j in range(3):
        absorb(z, j)
    loads[2].wait()
    for i in range(2):
        LT[384 + 128 * i:512 + 128 * i, :] = a_low[i].T
    came = []
    for s in range(last + 1):
        for j in range(3):
            for way in range(2):
                if not passes(way, s, j):
                    continue
                owner = row_of(-1 - s if way == 0 else 1 + s)
                hop(way, s, j, owner).wait_recv()
                if passes(way, s + 1, j):
                    hops.append(hop(way, s + 1, j, owner))
                    hops[-1].start()
                if came:
                    absorb(*came.pop())
                came.append((owner, j))
    absorb(*came.pop())

    part = jnp.zeros((128, B), f32)
    for j in range(3):
        square = pltpu.roll(ACC[j, 64:128, 256:384], 64, 1)
        square = jnp.where(low_lanes(64), square, 0.0).astype(bf16)
        square = jnp.concatenate([square, jnp.zeros((64, 128), bf16)], axis=0)
        own = nn(ROW[j, slab(z), :], square).astype(bf16)
        part = part + nn(own, LT[640 + 128 * j:768 + 128 * j, :])
    DP[...] = part.astype(bf16).reshape(4, 2, 16, B)

    def all_in(ref, sem):
        pltpu.make_async_copy(ref, ref, sem).wait()

    diag_swap = pltpu.make_async_remote_copy(
        src_ref=DP.at[:, 1 - core], dst_ref=DX, send_sem=dsend.at[0], recv_sem=drecv.at[0],
        device_id=other, device_id_type=MESH,
    )
    diag_swap.start()

    def place_of(owner):
        pair = lax.rem(owner, 4)
        return pair, lax.rem(pair + lax.div(owner, 4), NC // strips)

    def columns_of(group):
        return pl.ds(pl.multiple_of(group * wide, 128), wide)

    weight = []
    for i in range(2):
        for j in range(3):
            block = ACC[j, :, 128 * i:128 * i + 128] * mask[i, j].astype(f32)
            flat = jnp.where(low_lanes(64), pltpu.roll(block[64:, :], 64, 1), 0.0).astype(bf16)
            m = 3 * i + j
            turned = block.T[64:, :]
            if m % 2 == 0:
                turned = jnp.where(low_lanes(64), pltpu.roll(turned, 64, 1), 0.0)
            else:
                turned = jnp.where(low_lanes(64), 0.0, turned)
            weight.append(jnp.concatenate([turned.astype(bf16), jnp.zeros((64, 128), bf16)], axis=0))
            LT[64 * m:64 * m + 64, :] = nt(flat, panel[i, j]).astype(bf16)
    for t in range(3):
        m, n = 2 * t, 2 * t + 1
        MIX[:, 128 * t:128 * t + 128] = (
            nn(panel[m // 3, m % 3], weight[m]) + nn(panel[n // 3, n % 3], weight[n])
        ).astype(bf16)

    def spread(inner):
        keep = low_lanes(192)
        zero = jnp.zeros_like(inner)
        return jnp.concatenate([jnp.where(keep, inner, zero), jnp.where(keep, zero, inner)], axis=0)

    def send_sum(n, terms):
        TS[n] = terms.reshape(half, 2, share, 128)
        copy = pltpu.make_async_remote_copy(
            src_ref=TS.at[n, :, 1 - core], dst_ref=XS.at[n], send_sem=xsend.at[n], recv_sem=xrecv.at[n],
            device_id=other, device_id_type=MESH,
        )
        copy.start()
        return copy

    def pass_sum(n, copy):
        copy.wait_recv()
        YS[n] = (TS[n, :, core] + XS[n]).astype(bf16)

        def send(d):
            pltpu.make_async_remote_copy(
                src_ref=YS.at[n, chip_of(d)], dst_ref=RS.at[n, d - 1],
                send_sem=rsend.at[n], recv_sem=rrecv.at[n],
                device_id={"cols": col_of(2 * d)}, device_id_type=MESH,
            ).start()

        each(half, send)

    def end_sum(n):
        all_in(RS.at[n], rrecv.at[n])
        return TS[n, chip, core] + XS[n, chip] + jnp.sum(RS[n].astype(f32), axis=0)

    def start_gather(n, whole, own):
        place = whole.at[chip, core]
        place[...] = own

        def send(d):
            pltpu.make_async_remote_copy(
                src_ref=place, dst_ref=place, send_sem=asend.at[n], recv_sem=arecv.at[n],
                device_id={"cols": col_of(2 * d)}, device_id_type=MESH,
            ).start()

        each(half, send)

    def end_gather(n, whole):
        all_in(whole.at[pl.ds(0, half - 1), core], arecv.at[n])
        place = whole.at[:, core]
        copy = pltpu.make_async_remote_copy(
            src_ref=place, dst_ref=place, send_sem=bsend.at[n], recv_sem=brecv.at[n],
            device_id=other, device_id_type=MESH,
        )
        copy.start()
        copy.wait_recv()
        return whole[...].reshape(B, 128)

    def low_rows(inner, up, rows):
        total = jnp.zeros((rows.size, 128), f32)
        zero = jnp.zeros((64, 128), bf16)
        for i in range(2):
            half = inner[128 * i + 64:128 * i + 128] if up else inner[128 * i:128 * i + 64]
            keep = low_lanes(64) if i == 0 else jnp.logical_not(low_lanes(64))
            half = jnp.where(keep, half, 0.0).astype(bf16)
            right = jnp.concatenate([half, zero] if up else [zero, half], axis=0)
            total = total + nn(a_low[i, rows, :], right)
        return total

    def back_terms(back):
        zero = jnp.zeros((64, 128), bf16)
        total = jnp.zeros((B, 128), f32)
        for j in range(3):
            mine = jnp.where(low_lanes(64), back[64 * j:64 * j + 64], back[192 + 64 * j:256 + 64 * j])
            total = total + nn(ROW[j], jnp.concatenate([mine.astype(bf16), zero], axis=0))
        return total

    nb = B // 128
    pair, group = place_of(chip)
    columns = columns_of(group)

    def to_chip(d, k):
        place = FULL.at[pl.ds(2 * k, 2), pair, core, :, columns]
        return pltpu.make_async_remote_copy(
            src_ref=place, dst_ref=place, send_sem=csend.at[k, d - 1], recv_sem=crecv.at[k, d - 1],
            device_id={"cols": col_of(2 * d)}, device_id_type=MESH,
        )

    def counts(owner, k):
        return (place_of(owner)[1] + 1) * wide > 256 * k

    def spread_group(k):
        @pl.when(counts(chip, k))
        def _():
            each(half, lambda d: to_chip(d, k).start())

    def to_core(k):
        place = FULL.at[pl.ds(2 * k, 2), :, core, :, pl.ds(256 * k, B - 256 * k)]
        return pltpu.make_async_remote_copy(
            src_ref=place, dst_ref=place, send_sem=dsend.at[3 + k], recv_sem=drecv.at[3 + k],
            device_id=other, device_id_type=MESH,
        )

    def pass_on(k):
        def take(d):
            @pl.when(counts(chip_of(half - d), k))
            def _():
                to_chip(d, k).wait_recv()

        each(half, take)
        to_core(k).start()

    def block_step(kb):
        o = kb * 128
        rest = o + 128
        top = FULL[kb].reshape(128, B)[:, o:].astype(f32)
        if kb:
            top = top + A[o:rest, o:]
        U, E = yield from chol_block(top[:, :128], 128, 16)
        A[o:rest, o:rest] = U
        Eb = E.astype(bf16)
        INV[kb] = Eb
        if rest < B:
            across = nn(Eb, top[:, 128:].astype(bf16))
            A[o:rest, rest:] = across
            ab = across.astype(bf16)
            LOW[rest:, o:rest] = ab.T
            yield
            for ib in range(kb + 1, nb):
                r = ib * 128
                gone = nn(LOW[r:r + 128, o:rest], ab[:, r - rest:])
                A[r:r + 128, r:] = A[r:r + 128, r:] - gone if kb else -gone
        block = A[o:rest, slab(z)].T
        row = z * 128 + lax.broadcasted_iota(jnp.int32, (128, 128), 0)
        col = o + lax.broadcasted_iota(jnp.int32, (128, 128), 1)
        slab_ref[:, o:rest] = jnp.where(col <= row, block, 0.0)

    to_do = list(range(nb))

    def some_steps(n):
        for _ in range(n):
            if to_do:
                together(block_step(to_do.pop(0)))

    diag_swap.wait_recv()
    DY[...] = (DP[:, core].astype(f32) + DX[...].astype(f32)).astype(bf16)

    def send_diag(d):
        to_pair, to_group = place_of(chip_of(d))
        pltpu.make_async_remote_copy(
            src_ref=DY.at[to_pair, :, columns_of(to_group)], dst_ref=DRS.at[d - 1],
            send_sem=dsend.at[1], recv_sem=drecv.at[1],
            device_id={"cols": col_of(2 * d)}, device_id_type=MESH,
        ).start()

    probe = jnp.concatenate([ACC[j, :64, 384:512] for j in range(3)], axis=0)
    x = send_sum(0, nn(MIX[...], spread(probe).astype(bf16)))
    low = low_rows(nn(LT[384:640, :], S2[...]), True, mine)
    each(half, send_diag)
    pass_sum(0, x)
    loads[3].wait()
    all_in(DRS, drecv.at[1])
    rows = pl.ds(pl.multiple_of((2 * pair + core) * 16, 16), 16)
    own = a_diag[rows, columns] - (
        DY[pair, :, columns].astype(f32) + jnp.sum(DRS[...].astype(f32), axis=0)
    )
    FULL[z, pair, core, :, columns] = own.astype(bf16)

    def send_rows(d):
        place = FULL.at[z, pair, core, :, columns]
        pltpu.make_async_remote_copy(
            src_ref=place, dst_ref=place, send_sem=dsend.at[2], recv_sem=drecv.at[2],
            device_id={"rows": row_of(d)}, device_id_type=MESH,
        ).start()

    each(NR, send_rows)
    start_gather(0, FB, (low - end_sum(0)).astype(bf16))
    all_in(FULL.at[pl.ds(0, NR - 1), pair, core, :, columns], drecv.at[2])
    spread_group(0)
    first = end_gather(0, FB)

    inner = nn(LT[:640, :], first)
    x = send_sum(1, back_terms(inner[:384]))
    low = low_rows(inner[384:], False, mine)
    pass_sum(1, x)
    pass_on(0)
    for k in range(1, nb // 2):
        spread_group(k)
    to_core(0).wait_recv()
    some_steps(1)
    start_gather(1, SB, (low - end_sum(1)).astype(bf16))
    some_steps(1)
    second = end_gather(1, SB)

    inner = nn(LT[384:, :], second)
    fore = jnp.concatenate([inner[256 + 128 * j:320 + 128 * j] for j in range(3)], axis=0)
    x = send_sum(2, nn(MIX[...], spread(fore).astype(bf16)))
    pass_sum(2, x)
    pass_on(1)
    low = low_rows(inner[:256], True, pl.ds(0, B))
    to_core(1).wait_recv()
    some_steps(1)
    start_gather(2, TH, end_sum(2).astype(bf16))
    for k in range(2, nb // 2):
        pass_on(k)
    some_steps(1)
    third = low - end_gather(2, TH).astype(f32)
    for k in range(2, nb // 2):
        to_core(k).wait_recv()

    gram = nn(third.T, third, HIGHEST)
    if to_do:
        inverse, _ = together(inverse_pair(gram), block_step(to_do.pop(0)))
    else:
        inverse, = together(inverse_pair(gram))
    basis = nt(third, inverse, HIGHEST)
    BS[...] = basis

    inner = nn(LT[:640, :], basis.astype(bf16))
    x = send_sum(3, back_terms(inner[:384]))
    low = low_rows(inner[384:], False, mine)
    pass_sum(3, x)
    some_steps(1)
    start_gather(3, PB, (low - end_sum(3)).astype(bf16))
    some_steps(nb)
    leaving = [pltpu.make_async_copy(slab_ref, slab_out, osem.at[nb])]
    leaving[0].start()
    Y[...] = end_gather(3, PB).astype(f32)

    left = low_lanes(128)
    for kb in range(nb):
        o = kb * 128
        y = nn(INV[kb], Y[o:o + 128, :].astype(bf16))
        if o + 128 < B:
            Y[o + 128:, :] -= nn(LOW[o + 128:, o:o + 128], y.astype(bf16))
        cols = BS[o:o + 128, :]
        panel_ref[0, o:o + 128, :] = jnp.where(left, cols, pltpu.roll(y, 64, 1))
        panel_ref[1, o:o + 128, :] = jnp.where(left, pltpu.roll(cols, 64, 1), y)
        made = pl.ds(o, 128)
        leaving.append(pltpu.make_async_copy(panel_ref.at[:, made], panel_out.at[:, made], osem.at[kb]))
        leaving[-1].start()

    for copy in leaving:
        copy.wait()
    for h in hops:
        h.wait_send()
    diag_swap.wait_send()
    all_in(DRS, dsend.at[1])
    all_in(FULL.at[pl.ds(0, NR - 1), pair, core, :, columns], dsend.at[2])
    for k in range(nb // 2):
        @pl.when(counts(chip, k))
        def _():
            each(half, lambda d: to_chip(d, k).wait_send())
        to_core(k).wait_send()
    for n, whole in enumerate((FB, SB, TH, PB)):
        all_in(XS.at[n], xsend.at[n])
        all_in(RS.at[n], rsend.at[n])
        all_in(whole.at[pl.ds(0, half - 1), core], asend.at[n])
        all_in(whole.at[:, core], bsend.at[n])


def out_kernel(panel_in, slab_in, panel_out, slab_out, panel_here, slab_here, into, out):
    parts = []
    size = panel_in.shape[1] // 4
    for n in range(4):
        cut = pl.ds(size * n, size)
        for i in range(2):
            parts.append([ref.at[i, cut] for ref in (panel_in, panel_here, panel_out)])
        cut = pl.ds(32 * n, 32)
        parts.append([ref.at[cut] for ref in (slab_in, slab_here, slab_out)])
    loads = [pltpu.make_async_copy(a, b, into.at[n]) for n, (a, b, _) in enumerate(parts)]
    stores = [pltpu.make_async_copy(b, c, out.at[n]) for n, (_, b, c) in enumerate(parts)]
    for copy in loads:
        copy.start()
    for load, store in zip(loads, stores):
        load.wait()
        store.start()
    for copy in stores:
        copy.wait()


def written(panel_out, slab):
    anywhere = pl.BlockSpec(memory_space=pl.ANY)
    return pl.pallas_call(
        out_kernel,
        out_shape=(jax.ShapeDtypeStruct(panel_out.shape, f32), jax.ShapeDtypeStruct(slab.shape, f32)),
        in_specs=[anywhere] * 2,
        out_specs=[anywhere] * 2,
        scratch_shapes=[
            pltpu.VMEM(panel_out.shape, f32), pltpu.VMEM(slab.shape, f32),
            pltpu.SemaphoreType.DMA((12,)), pltpu.SemaphoreType.DMA((12,)),
        ],
        compiler_params=pltpu.CompilerParams(vmem_limit_bytes=60 * 2**20),
        name="written",
    )(panel_out, slab)


def shards(panel, row_k, mask, a_low, a_diag, sketch):
    NC, NR = lax.axis_size("cols"), lax.axis_size("rows")
    B = NR * 128
    share = B // NC
    half = NC // 2
    wide = B // (NC // 8)
    vm = pl.BlockSpec(memory_space=pltpu.VMEM)
    anywhere = pl.BlockSpec(memory_space=pl.ANY)
    dma = pltpu.SemaphoreType.DMA
    shape = jax.ShapeDtypeStruct
    outs = pl.pallas_call(
        functools.partial(panel_kernel, NC=NC, NR=NR),
        out_shape=(shape((2, B, 128), f32), shape((128, B), f32)),
        in_specs=[anywhere, anywhere, pl.BlockSpec(memory_space=pltpu.SMEM), anywhere, anywhere, vm],
        out_specs=[anywhere] * 2,
        scratch_shapes=[
            pltpu.VMEM((2, B, 128), f32),
            pltpu.VMEM((128, B), f32),
            pltpu.VMEM((2, 3, B, 128), bf16),
            pltpu.VMEM((2, B, 128), bf16),
            pltpu.VMEM((128, B), f32),
            pltpu.VMEM((3, B, 128), bf16),
            pltpu.VMEM((1024, B), bf16),
            pltpu.VMEM((3, 128, 512), f32),
            pltpu.VMEM((B, 384), bf16),
            pltpu.VMEM((B, 128), bf16),
            pltpu.VMEM((4, 2, 16, B), bf16),
            pltpu.VMEM((4, 16, B), bf16),
            pltpu.VMEM((4, 16, B), bf16),
            pltpu.VMEM((half - 1, 16, wide), bf16),
            pltpu.VMEM((NR, 4, 2, 16, B), bf16),
            pltpu.VMEM((4, half, 2, share, 128), f32),
            pltpu.VMEM((4, half, share, 128), f32),
            pltpu.VMEM((4, half, share, 128), bf16),
            pltpu.VMEM((4, half - 1, share, 128), bf16),
            pltpu.VMEM((half, 2, share, 128), bf16),
            pltpu.VMEM((half, 2, share, 128), bf16),
            pltpu.VMEM((half, 2, share, 128), bf16),
            pltpu.VMEM((half, 2, share, 128), bf16),
            pltpu.VMEM((B, 128), f32),
            pltpu.VMEM((B, B), f32),
            pltpu.VMEM((B, B), bf16),
            pltpu.VMEM((NR, 128, 128), bf16),
            pltpu.VMEM((B, 128), f32),
            dma((4,)), dma((NR + 1,)), dma((2, 4, 3)), dma((2, 4, 3)), dma((3 + NR // 2,)), dma((3 + NR // 2,)),
            dma((NR // 2, half)), dma((NR // 2, half)),
            dma((4,)), dma((4,)), dma((4,)), dma((4,)), dma((4,)), dma((4,)), dma((4,)), dma((4,)),
        ],
        compiler_params=pltpu.CompilerParams(
            collective_id=0, has_side_effects=True, vmem_limit_bytes=56 * 2**20
        ),
        name="panel",
    )(panel, row_k, mask, a_low, a_diag, sketch.T)
    return written(*outs)


def solution(mesh):
    return jax.shard_map(
        shards,
        mesh=mesh,
        in_specs=(
            P("rows", "cols", None, None),
            P("cols", "rows", None),
            P("rows", "cols"),
            P("rows", None, None),
            P("rows", None),
            P(),
        ),
        out_specs=(P("rows", None, None), P("rows", None)),
        check_vma=False,
    )
```

```python
import functools

import jax
import jax.numpy as jnp
from jax import lax
from jax.experimental import pallas as pl
from jax.experimental.pallas import tpu as pltpu
from jax.sharding import PartitionSpec as P

f32 = jnp.float32
bf16 = jnp.bfloat16
MESH = pl.DeviceIdType.MESH
HIGHEST = lax.Precision.HIGHEST

def rcp(p):
    r = pl.reciprocal(p, approx=True)
    return r * (2.0 - p * r)

def strip_eliminate(parts, k0, s):
    first = parts[0]
    lanes = first.shape[1]
    row = lax.broadcasted_iota(jnp.int32, (s, lanes), 0)
    C = [jnp.broadcast_to(first[:, k0 + j:k0 + j + 1], (s, lanes)) for j in range(s)]
    parts = list(parts)
    diag = jnp.ones((s, lanes), f32)

    def spread(x, n):
        return jnp.broadcast_to(x[n:n + 1, :], (8, lanes))

    def tall(x):
        return jnp.concatenate([x] * (s // 8), axis=0)

    p = spread(C[0], 0)
    for j in range(s):
        diag = jnp.where(row == j, tall(p), diag)
        if j == s - 1:
            break
        below = jnp.where(row > j, C[j], 0.0)
        w = spread(C[j], j + 1) * spread(C[j + 1], j)
        q = spread(C[j + 1], j + 1)
        r = pl.reciprocal(p, approx=True)
        u = 2.0 - p * r
        p = q - (w * r) * u
        M = (below * tall(r)) * tall(u)
        for k in range(j + 1, s):
            C[k] = C[k] - M * C[k][j:j + 1, :]
        parts = [x - M * x[j:j + 1, :] for x in parts]
    R = lax.rsqrt(diag)
    return [x * R for x in parts]


def tn(a, b, prec=None):
    return lax.dot_general(a, b, (((0,), (0,)), ((), ())), preferred_element_type=f32, precision=prec)

def chol_block(D, n, s):
    eye = (lax.broadcasted_iota(jnp.int32, (n, n), 0) == lax.broadcasted_iota(jnp.int32, (n, n), 1)).astype(f32)
    WA, WE = D, eye
    outU, outE = [], []
    for k0 in range(0, n, s):
        a, e = strip_eliminate([WA[:s], WE[:s]], k0, s)
        outU.append(a)
        outE.append(e)
        if k0 + s < n:
            ab = a.astype(bf16)
            eb = e.astype(bf16)
            lhs = ab[:, k0 + s:]
            WA = WA[s:] - tn(lhs, ab)
            WE = WE[s:] - tn(lhs, eb)
            yield
    U = jnp.concatenate(outU, 0)
    E = jnp.concatenate(outE, 0)
    i0 = lax.broadcasted_iota(jnp.int32, (n, n), 0)
    i1 = lax.broadcasted_iota(jnp.int32, (n, n), 1)
    return jnp.where(i1 >= i0, U, 0.0), E


def together(*works):
    given = [None] * len(works)
    live = list(range(len(works)))
    while live:
        for n in list(live):
            try:
                next(works[n])
            except StopIteration as stop:
                given[n] = stop.value
                live.remove(n)
    return given


def inverse_pair(gram):
    n, s = 64, 16
    low = lax.broadcasted_iota(jnp.int32, (s, 128), 1) < n
    row = lax.broadcasted_iota(jnp.int32, (s, 128), 0)
    lanes = lax.broadcasted_iota(jnp.int32, (n, 128), 1)
    left = lanes < n
    A = jnp.where(left, gram[:n], gram[n:])
    E = (lax.rem(lanes, n) == lax.broadcasted_iota(jnp.int32, (n, 128), 0)).astype(f32)
    done = []
    for k0 in range(0, n, s):
        a, e = A[:s], E[:s]
        C = [
            jnp.where(
                low,
                jnp.broadcast_to(a[:, k0 + j:k0 + j + 1], (s, 128)),
                jnp.broadcast_to(a[:, n + k0 + j:n + k0 + j + 1], (s, 128)),
            )
            for j in range(s)
        ]
        diag = jnp.ones((s, 128), f32)
        for j in range(s):
            p = C[j][j:j + 1, :]
            diag = jnp.where(row == j, p, diag)
            if j == s - 1:
                break
            r = rcp(p)
            r = r * (2.0 - p * r)
            M = jnp.where(row > j, C[j] * r, 0.0)
            for k in range(j + 1, s):
                C[k] = C[k] - M * C[k][j:j + 1, :]
            a = a - M * a[j:j + 1, :]
            e = e - M * e[j:j + 1, :]
        R = lax.rsqrt(diag)
        a, e = a * R, e * R
        done.append(e)
        if k0 + s < n:
            both = tn(a, jnp.concatenate([a, e], axis=1), HIGHEST)
            both = [both[:, :128], both[:, 128:]]
            keep = left[k0 + s:]
            step = [jnp.where(keep, x[k0 + s:n], x[n + k0 + s:]) for x in both]
            A, E = A[s:] - step[0], E[s:] - step[1]
            yield
    E = jnp.concatenate(done, axis=0)
    return jnp.concatenate([jnp.where(left, E, 0.0), jnp.where(left, 0.0, E)], axis=0)


def nn(a, b, prec=None):
    return jnp.dot(a, b, preferred_element_type=f32, precision=prec)


def nt(a, b, prec=None):
    return lax.dot_general(a, b, (((1,), (1,)), ((), ())), preferred_element_type=f32, precision=prec)


def low_lanes(n):
    return lax.broadcasted_iota(jnp.int32, (n, 128), 1) < 64


def panel_kernel(
    panel_in, row_in, mask, low_in, diag_in, sketch,
    panel_out, slab_out,
    panel_ref, slab_ref, panel, a_low, a_diag, ROW, LT, ACC, MIX, S2, DP, DX, DY, DRS, FULL, TS, XS, YS, RS, FB, SB, TH, PB, BS,
    A, LOW, INV, Y,
    lsem, osem, zsend, zrecv, dsend, drecv, csend, crecv, xsend, xrecv, rsend, rrecv, asend, arecv, bsend, brecv,
    *, NC, NR,
):
    B = NR * 128
    share = B // NC
    half = NC // 2
    strips = 8
    wide = B // (NC // strips)
    c = lax.axis_index("cols")
    z = lax.axis_index("rows")
    core, chip = lax.rem(c, 2), lax.div(c, 2)
    mine = pl.ds(pl.multiple_of(c * share, share), share)
    other = {"cols": c + 1 - 2 * core}
    barrier = pltpu.get_barrier_semaphore()

    def col_of(d):
        return lax.rem(c + d, NC)

    def chip_of(d):
        return lax.rem(chip + d, half)

    def row_of(d):
        return lax.rem(z + d + NR, NR)

    def slab(owner):
        return pl.ds(pl.multiple_of(owner * 128, 128), 128)

    def each(n, body):
        def step(d, carry):
            body(d)
            return carry
        lax.fori_loop(1, n, step, 0)

    loads = [
        pltpu.make_async_copy(row_in, ROW.at[:, slab(z), :], lsem.at[0]),
        pltpu.make_async_copy(panel_in, panel, lsem.at[1]),
        pltpu.make_async_copy(low_in, a_low, lsem.at[2]),
        pltpu.make_async_copy(diag_in, a_diag, lsem.at[3]),
    ]
    for load in loads:
        load.start()
    each(half, lambda d: pl.semaphore_signal(barrier, 1, device_id={"cols": col_of(2 * d)}, device_id_type=MESH))
    pl.semaphore_signal(barrier, 1, device_id=other, device_id_type=MESH)
    each(NR, lambda d: pl.semaphore_signal(barrier, 1, device_id={"rows": row_of(d)}, device_id_type=MESH))
    S2[...] = jnp.concatenate([sketch[...], sketch[...]], axis=0).T
    for j in range(3):
        ACC[j] = jnp.zeros_like(ACC[j])
    loads[0].wait()
    pl.semaphore_wait(barrier, half + NR - 1)

    def hop(way, step, j, owner):
        place = ROW.at[j, slab(owner), :]
        return pltpu.make_async_remote_copy(
            src_ref=place, dst_ref=place,
            send_sem=zsend.at[way, step, j], recv_sem=zrecv.at[way, step, j],
            device_id={"rows": row_of(1 if way == 0 else -1)}, device_id_type=MESH,
        )

    def absorb(owner, j):
        r = ROW[j, slab(owner), :]
        rt = r.T
        LT[640 + 128 * j:768 + 128 * j, slab(owner)] = rt
        right = jnp.concatenate(
            [panel[0, j, slab(owner), :], panel[1, j, slab(owner), :], r, S2[slab(owner), :]], axis=1
        )
        ACC[j] += nn(rt, right)

    last = NR // 2 - 1

    def passes(way, step, j):
        return step < last or (step == last and (way == 0) == (j < 2))

    hops = []
    for j in range(3):
        for way in range(2):
            if passes(way, 0, j):
                hops.append(hop(way, 0, j, z))
                hops[-1].start()
    loads[1].wait()
    for j in range(3):
        absorb(z, j)
    loads[2].wait()
    for i in range(2):
        LT[384 + 128 * i:512 + 128 * i, :] = a_low[i].T
    came = []
    for s in range(last + 1):
        for j in range(3):
            for way in range(2):
                if not passes(way, s, j):
                    continue
                owner = row_of(-1 - s if way == 0 else 1 + s)
                hop(way, s, j, owner).wait_recv()
                if passes(way, s + 1, j):
                    hops.append(hop(way, s + 1, j, owner))
                    hops[-1].start()
                if came:
                    absorb(*came.pop())
                came.append((owner, j))
    absorb(*came.pop())

    part = jnp.zeros((128, B), f32)
    for j in range(3):
        square = pltpu.roll(ACC[j, 64:128, 256:384], 64, 1)
        square = jnp.where(low_lanes(64), square, 0.0).astype(bf16)
        square = jnp.concatenate([square, jnp.zeros((64, 128), bf16)], axis=0)
        own = nn(ROW[j, slab(z), :], square).astype(bf16)
        part = part + nn(own, LT[640 + 128 * j:768 + 128 * j, :])
    DP[...] = part.astype(bf16).reshape(4, 2, 16, B)

    def all_in(ref, sem):
        pltpu.make_async_copy(ref, ref, sem).wait()

    diag_swap = pltpu.make_async_remote_copy(
        src_ref=DP.at[:, 1 - core], dst_ref=DX, send_sem=dsend.at[0], recv_sem=drecv.at[0],
        device_id=other, device_id_type=MESH,
    )
    diag_swap.start()

    def place_of(owner):
        pair = lax.rem(owner, 4)
        return pair, lax.rem(pair + lax.div(owner, 4), NC // strips)

    def columns_of(group):
        return pl.ds(pl.multiple_of(group * wide, 128), wide)

    weight = []
    for i in range(2):
        for j in range(3):
            block = ACC[j, :, 128 * i:128 * i + 128] * mask[i, j].astype(f32)
            flat = jnp.where(low_lanes(64), pltpu.roll(block[64:, :], 64, 1), 0.0).astype(bf16)
            m = 3 * i + j
            turned = block.T[64:, :]
            if m % 2 == 0:
                turned = jnp.where(low_lanes(64), pltpu.roll(turned, 64, 1), 0.0)
            else:
                turned = jnp.where(low_lanes(64), 0.0, turned)
            weight.append(jnp.concatenate([turned.astype(bf16), jnp.zeros((64, 128), bf16)], axis=0))
            LT[64 * m:64 * m + 64, :] = nt(flat, panel[i, j]).astype(bf16)
    for t in range(3):
        m, n = 2 * t, 2 * t + 1
        MIX[:, 128 * t:128 * t + 128] = (
            nn(panel[m // 3, m % 3], weight[m]) + nn(panel[n // 3, n % 3], weight[n])
        ).astype(bf16)

    def spread(inner):
        keep = low_lanes(192)
        zero = jnp.zeros_like(inner)
        return jnp.concatenate([jnp.where(keep, inner, zero), jnp.where(keep, zero, inner)], axis=0)

    def send_sum(n, terms):
        TS[n] = terms.reshape(half, 2, share, 128)
        copy = pltpu.make_async_remote_copy(
            src_ref=TS.at[n, :, 1 - core], dst_ref=XS.at[n], send_sem=xsend.at[n], recv_sem=xrecv.at[n],
            device_id=other, device_id_type=MESH,
        )
        copy.start()
        return copy

    def pass_sum(n, copy):
        copy.wait_recv()
        YS[n] = (TS[n, :, core] + XS[n]).astype(bf16)

        def send(d):
            pltpu.make_async_remote_copy(
                src_ref=YS.at[n, chip_of(d)], dst_ref=RS.at[n, d - 1],
                send_sem=rsend.at[n], recv_sem=rrecv.at[n],
                device_id={"cols": col_of(2 * d)}, device_id_type=MESH,
            ).start()

        each(half, send)

    def end_sum(n):
        all_in(RS.at[n], rrecv.at[n])
        return TS[n, chip, core] + XS[n, chip] + jnp.sum(RS[n].astype(f32), axis=0)

    def start_gather(n, whole, own):
        place = whole.at[chip, core]
        place[...] = own

        def send(d):
            pltpu.make_async_remote_copy(
                src_ref=place, dst_ref=place, send_sem=asend.at[n], recv_sem=arecv.at[n],
                device_id={"cols": col_of(2 * d)}, device_id_type=MESH,
            ).start()

        each(half, send)

    def end_gather(n, whole, meanwhile=lambda: None):
        all_in(whole.at[pl.ds(0, half - 1), core], arecv.at[n])
        place = whole.at[:, core]
        copy = pltpu.make_async_remote_copy(
            src_ref=place, dst_ref=place, send_sem=bsend.at[n], recv_sem=brecv.at[n],
            device_id=other, device_id_type=MESH,
        )
        copy.start()
        meanwhile()
        copy.wait_recv()
        return whole[...].reshape(B, 128)

    def low_rows(inner, up, rows):
        total = jnp.zeros((rows.size, 128), f32)
        zero = jnp.zeros((64, 128), bf16)
        for i in range(2):
            half = inner[128 * i + 64:128 * i + 128] if up else inner[128 * i:128 * i + 64]
            keep = low_lanes(64) if i == 0 else jnp.logical_not(low_lanes(64))
            half = jnp.where(keep, half, 0.0).astype(bf16)
            right = jnp.concatenate([half, zero] if up else [zero, half], axis=0)
            total = total + nn(a_low[i, rows, :], right)
        return total

    def back_terms(back):
        zero = jnp.zeros((64, 128), bf16)
        total = jnp.zeros((B, 128), f32)
        for j in range(3):
            mine = jnp.where(low_lanes(64), back[64 * j:64 * j + 64], back[192 + 64 * j:256 + 64 * j])
            total = total + nn(ROW[j], jnp.concatenate([mine.astype(bf16), zero], axis=0))
        return total

    nb = B // 128
    pair, group = place_of(chip)
    columns = columns_of(group)

    def to_chip(d, k):
        place = FULL.at[pl.ds(2 * k, 2), pair, core, :, columns]
        return pltpu.make_async_remote_copy(
            src_ref=place, dst_ref=place, send_sem=csend.at[k, d - 1], recv_sem=crecv.at[k, d - 1],
            device_id={"cols": col_of(2 * d)}, device_id_type=MESH,
        )

    def counts(owner, k):
        return (place_of(owner)[1] + 1) * wide > 256 * k

    def spread_group(k):
        @pl.when(counts(chip, k))
        def _():
            each(half, lambda d: to_chip(d, k).start())

    def to_core(k):
        place = FULL.at[pl.ds(2 * k, 2), :, core, :, pl.ds(256 * k, B - 256 * k)]
        return pltpu.make_async_remote_copy(
            src_ref=place, dst_ref=place, send_sem=dsend.at[3 + k], recv_sem=drecv.at[3 + k],
            device_id=other, device_id_type=MESH,
        )

    def pass_on(k):
        def take(d):
            @pl.when(counts(chip_of(half - d), k))
            def _():
                to_chip(d, k).wait_recv()

        each(half, take)
        to_core(k).start()

    def block_step(kb):
        o = kb * 128
        rest = o + 128
        top = FULL[kb].reshape(128, B)[:, o:].astype(f32)
        if kb:
            top = top + A[o:rest, o:]
        U, E = yield from chol_block(top[:, :128], 128, 16)
        A[o:rest, o:rest] = U
        Eb = E.astype(bf16)
        INV[kb] = Eb
        if rest < B:
            across = nn(Eb, top[:, 128:].astype(bf16))
            A[o:rest, rest:] = across
            ab = across.astype(bf16)
            LOW[rest:, o:rest] = ab.T
            yield
            for ib in range(kb + 1, nb):
                r = ib * 128
                gone = nn(LOW[r:r + 128, o:rest], ab[:, r - rest:])
                A[r:r + 128, r:] = A[r:r + 128, r:] - gone if kb else -gone
        block = A[o:rest, slab(z)].T
        row = z * 128 + lax.broadcasted_iota(jnp.int32, (128, 128), 0)
        col = o + lax.broadcasted_iota(jnp.int32, (128, 128), 1)
        slab_ref[:, o:rest] = jnp.where(col <= row, block, 0.0)

    def all_steps():
        for kb in range(nb):
            yield from block_step(kb)
            yield

    work = all_steps()

    def in_turns(n):
        for _ in range(n):
            next(work, None)
            yield

    def advance(n):
        for _ in in_turns(n):
            pass

    diag_swap.wait_recv()
    DY[...] = (DP[:, core].astype(f32) + DX[...].astype(f32)).astype(bf16)

    def send_diag(d):
        to_pair, to_group = place_of(chip_of(d))
        pltpu.make_async_remote_copy(
            src_ref=DY.at[to_pair, :, columns_of(to_group)], dst_ref=DRS.at[d - 1],
            send_sem=dsend.at[1], recv_sem=drecv.at[1],
            device_id={"cols": col_of(2 * d)}, device_id_type=MESH,
        ).start()

    probe = jnp.concatenate([ACC[j, :64, 384:512] for j in range(3)], axis=0)
    x = send_sum(0, nn(MIX[...], spread(probe).astype(bf16)))
    low = low_rows(nn(LT[384:640, :], S2[...]), True, mine)
    each(half, send_diag)
    pass_sum(0, x)
    loads[3].wait()
    all_in(DRS, drecv.at[1])
    rows = pl.ds(pl.multiple_of((2 * pair + core) * 16, 16), 16)
    own = a_diag[rows, columns] - (
        DY[pair, :, columns].astype(f32) + jnp.sum(DRS[...].astype(f32), axis=0)
    )
    FULL[z, pair, core, :, columns] = own.astype(bf16)

    def send_rows(d):
        place = FULL.at[z, pair, core, :, columns]
        pltpu.make_async_remote_copy(
            src_ref=place, dst_ref=place, send_sem=dsend.at[2], recv_sem=drecv.at[2],
            device_id={"rows": row_of(d)}, device_id_type=MESH,
        ).start()

    each(NR, send_rows)
    start_gather(0, FB, (low - end_sum(0)).astype(bf16))
    all_in(FULL.at[pl.ds(0, NR - 1), pair, core, :, columns], drecv.at[2])
    spread_group(0)
    first = end_gather(0, FB)

    inner = nn(LT[:640, :], first)
    x = send_sum(1, back_terms(inner[:384]))
    low = low_rows(inner[384:], False, mine)
    pass_sum(1, x)
    pass_on(0)
    for k in range(1, nb // 2):
        spread_group(k)
    to_core(0).wait_recv()
    advance(7)
    start_gather(1, SB, (low - end_sum(1)).astype(bf16))
    advance(9)
    second = end_gather(1, SB, lambda: advance(2))

    inner = nn(LT[384:, :], second)
    fore = jnp.concatenate([inner[256 + 128 * j:320 + 128 * j] for j in range(3)], axis=0)
    x = send_sum(2, nn(MIX[...], spread(fore).astype(bf16)))
    pass_sum(2, x)
    pass_on(1)
    low = low_rows(inner[:256], True, pl.ds(0, B))
    to_core(1).wait_recv()
    advance(9)
    start_gather(2, TH, end_sum(2).astype(bf16))
    for k in range(2, nb // 2):
        pass_on(k)
    advance(7)
    third = low - end_gather(2, TH, lambda: advance(2)).astype(f32)
    for k in range(2, nb // 2):
        to_core(k).wait_recv()

    gram = nn(third.T, third, HIGHEST)
    inverse, _ = together(inverse_pair(gram), in_turns(9))
    basis = nt(third, inverse, HIGHEST)
    BS[...] = basis

    inner = nn(LT[:640, :], basis.astype(bf16))
    x = send_sum(3, back_terms(inner[:384]))
    low = low_rows(inner[384:], False, mine)
    advance(2)
    pass_sum(3, x)
    advance(9)
    start_gather(3, PB, (low - end_sum(3)).astype(bf16))
    advance(13)
    Y[...] = end_gather(3, PB, lambda: advance(9 * nb)).astype(f32)
    leaving = [pltpu.make_async_copy(slab_ref, slab_out, osem.at[nb])]
    leaving[0].start()

    left = low_lanes(128)
    for kb in range(nb):
        o = kb * 128
        y = nn(INV[kb], Y[o:o + 128, :].astype(bf16))
        if o + 128 < B:
            Y[o + 128:, :] -= nn(LOW[o + 128:, o:o + 128], y.astype(bf16))
        cols = BS[o:o + 128, :]
        panel_ref[0, o:o + 128, :] = jnp.where(left, cols, pltpu.roll(y, 64, 1))
        panel_ref[1, o:o + 128, :] = jnp.where(left, pltpu.roll(cols, 64, 1), y)
        made = pl.ds(o, 128)
        leaving.append(pltpu.make_async_copy(panel_ref.at[:, made], panel_out.at[:, made], osem.at[kb]))
        leaving[-1].start()

    for copy in leaving:
        copy.wait()
    for h in hops:
        h.wait_send()
    diag_swap.wait_send()
    all_in(DRS, dsend.at[1])
    all_in(FULL.at[pl.ds(0, NR - 1), pair, core, :, columns], dsend.at[2])
    for k in range(nb // 2):
        @pl.when(counts(chip, k))
        def _():
            each(half, lambda d: to_chip(d, k).wait_send())
        to_core(k).wait_send()
    for n, whole in enumerate((FB, SB, TH, PB)):
        all_in(XS.at[n], xsend.at[n])
        all_in(RS.at[n], rsend.at[n])
        all_in(whole.at[pl.ds(0, half - 1), core], asend.at[n])
        all_in(whole.at[:, core], bsend.at[n])


def out_kernel(panel_in, slab_in, panel_out, slab_out, panel_here, slab_here, into, out):
    parts = []
    size = panel_in.shape[1] // 4
    for n in range(4):
        cut = pl.ds(size * n, size)
        for i in range(2):
            parts.append([ref.at[i, cut] for ref in (panel_in, panel_here, panel_out)])
        cut = pl.ds(32 * n, 32)
        parts.append([ref.at[cut] for ref in (slab_in, slab_here, slab_out)])
    loads = [pltpu.make_async_copy(a, b, into.at[n]) for n, (a, b, _) in enumerate(parts)]
    stores = [pltpu.make_async_copy(b, c, out.at[n]) for n, (_, b, c) in enumerate(parts)]
    for copy in loads:
        copy.start()
    for load, store in zip(loads, stores):
        load.wait()
        store.start()
    for copy in stores:
        copy.wait()


def written(panel_out, slab):
    anywhere = pl.BlockSpec(memory_space=pl.ANY)
    return pl.pallas_call(
        out_kernel,
        out_shape=(jax.ShapeDtypeStruct(panel_out.shape, f32), jax.ShapeDtypeStruct(slab.shape, f32)),
        in_specs=[anywhere] * 2,
        out_specs=[anywhere] * 2,
        scratch_shapes=[
            pltpu.VMEM(panel_out.shape, f32), pltpu.VMEM(slab.shape, f32),
            pltpu.SemaphoreType.DMA((12,)), pltpu.SemaphoreType.DMA((12,)),
        ],
        compiler_params=pltpu.CompilerParams(vmem_limit_bytes=60 * 2**20),
        name="written",
    )(panel_out, slab)


def shards(panel, row_k, mask, a_low, a_diag, sketch):
    NC, NR = lax.axis_size("cols"), lax.axis_size("rows")
    B = NR * 128
    share = B // NC
    half = NC // 2
    wide = B // (NC // 8)
    vm = pl.BlockSpec(memory_space=pltpu.VMEM)
    anywhere = pl.BlockSpec(memory_space=pl.ANY)
    dma = pltpu.SemaphoreType.DMA
    shape = jax.ShapeDtypeStruct
    outs = pl.pallas_call(
        functools.partial(panel_kernel, NC=NC, NR=NR),
        out_shape=(shape((2, B, 128), f32), shape((128, B), f32)),
        in_specs=[anywhere, anywhere, pl.BlockSpec(memory_space=pltpu.SMEM), anywhere, anywhere, vm],
        out_specs=[anywhere] * 2,
        scratch_shapes=[
            pltpu.VMEM((2, B, 128), f32),
            pltpu.VMEM((128, B), f32),
            pltpu.VMEM((2, 3, B, 128), bf16),
            pltpu.VMEM((2, B, 128), bf16),
            pltpu.VMEM((128, B), f32),
            pltpu.VMEM((3, B, 128), bf16),
            pltpu.VMEM((1024, B), bf16),
            pltpu.VMEM((3, 128, 512), f32),
            pltpu.VMEM((B, 384), bf16),
            pltpu.VMEM((B, 128), bf16),
            pltpu.VMEM((4, 2, 16, B), bf16),
            pltpu.VMEM((4, 16, B), bf16),
            pltpu.VMEM((4, 16, B), bf16),
            pltpu.VMEM((half - 1, 16, wide), bf16),
            pltpu.VMEM((NR, 4, 2, 16, B), bf16),
            pltpu.VMEM((4, half, 2, share, 128), f32),
            pltpu.VMEM((4, half, share, 128), f32),
            pltpu.VMEM((4, half, share, 128), bf16),
            pltpu.VMEM((4, half - 1, share, 128), bf16),
            pltpu.VMEM((half, 2, share, 128), bf16),
            pltpu.VMEM((half, 2, share, 128), bf16),
            pltpu.VMEM((half, 2, share, 128), bf16),
            pltpu.VMEM((half, 2, share, 128), bf16),
            pltpu.VMEM((B, 128), f32),
            pltpu.VMEM((B, B), f32),
            pltpu.VMEM((B, B), bf16),
            pltpu.VMEM((NR, 128, 128), bf16),
            pltpu.VMEM((B, 128), f32),
            dma((4,)), dma((NR + 1,)), dma((2, 4, 3)), dma((2, 4, 3)), dma((3 + NR // 2,)), dma((3 + NR // 2,)),
            dma((NR // 2, half)), dma((NR // 2, half)),
            dma((4,)), dma((4,)), dma((4,)), dma((4,)), dma((4,)), dma((4,)), dma((4,)), dma((4,)),
        ],
        compiler_params=pltpu.CompilerParams(
            collective_id=0, has_side_effects=True, vmem_limit_bytes=56 * 2**20
        ),
        name="panel",
    )(panel, row_k, mask, a_low, a_diag, sketch.T)
    return written(*outs)


def solution(mesh):
    return jax.shard_map(
        shards,
        mesh=mesh,
        in_specs=(
            P("rows", "cols", None, None),
            P("cols", "rows", None),
            P("rows", "cols"),
            P("rows", None, None),
            P("rows", None),
            P(),
        ),
        out_specs=(P("rows", None, None), P("rows", None)),
        check_vma=False,
    )
```
